128 devices in a mesh: tensor: 8 (over x_lo, y), ulysses: 16 (over z, x_hi, core).
Axes of the slice: x: 4 (x_hi: 2, x_lo: 2; x = x_hi * 2 + x_lo), y: 4, z: 4, core: 2. Of those that a mesh axis runs over, the one named last changes fastest.
Arguments:
- tokens: bfloat16 [1024, 16384], P('ulysses'), may hold values from -6 to 6
- q_weight: bfloat16 [16384, 16384], P('ulysses', 'tensor'), may hold values from -0.046875 to 0.046875
- k_weight: bfloat16 [16384, 1024], P('ulysses', 'tensor'), may hold values from -0.046875 to 0.046875
- v_weight: bfloat16 [16384, 1024], P('ulysses', 'tensor'), may hold values from -0.046875 to 0.046875
- cache_keys: bfloat16 [16384, 1024], P('ulysses', 'tensor'), may hold values from -160 to 160
- cache_values: bfloat16 [16384, 1024], P('ulysses', 'tensor'), may hold values from -6 to 6
- cache_len: int32 [1], replicated, may hold values from 8192 to 16384
- span_start: int32 [1], replicated, may hold values from 16384 to 32767
Outputs:
- attended: bfloat16 [1024, 16384], P(('tensor', 'ulysses'))
The draws below stay inside these ranges and needn't reach their ends.
All inputs are finite; a program needn't handle non-finite values.
Results may differ from the reference program's by a relative error of at most 0.014.
The reference program's roundings to bfloat16 on the way count: a program that leaves them out, or rounds other values in their place, can miss the bound.
Values may be sent and summed in bfloat16 or wider, within the bound.
No kernel may reach another device: no remote copies, remote signals or barrier semaphores. Data moves between devices by JAX's collectives and lax.ppermute only.
A program may use at most 128 MiB of HBM per device.

```python
import math
import jax
import jax.numpy as jnp
from jax import lax

D = 16384
HEADS = 128
KV = 8
HD = 128
SPAN = 1024
CACHE = 16384


def draw_cache_keys(key, part):
    key = jax.random.fold_in(key, 11)
    first_key = jax.random.fold_in(key, 0)
    base = jax.random.truncated_normal(first_key, -4.0, 4.0, (CACHE, KV * HD), jnp.float32)
    return base.astype(jnp.bfloat16)


def shard_levels(own_key, extent, shards, smallest, top_value):
    def one(position, parts):
        draws = jax.random.uniform(jax.random.fold_in(jax.random.fold_in(own_key, 6), position), (parts,), jnp.float32, smallest / len(shards), top_value / len(shards))
        return jnp.repeat(jnp.exp(draws), extent[position] // parts).reshape((-1,) + (1,) * (len(extent) - position - 1))

    gain = one(*shards[0])
    for cut in shards[1:]:
        gain = gain * one(*cut)
    return gain


def normal_values(rng, extent, width, most, cuts=(), held_as=jnp.bfloat16):
    factor_of = shard_levels(rng, extent, cuts, -0.22, 0.18) if cuts else 1.0
    entries = jax.random.normal(rng, extent, jnp.float32) * width * factor_of
    return jnp.minimum(jnp.maximum(entries, -most), most).astype(held_as)


def setup_inputs(seed: int = 0) -> dict:
    key_list = jax.random.split(jax.random.key(seed), 9)
    tokens = normal_values(key_list[0], (SPAN, D), 1.0, 6.0, ((0, 16),))
    q_weight = normal_values(key_list[1], (D, HEADS * HD), D ** -0.5, 0.046875, ((0, 16), (1, 8)))
    k_weight = normal_values(key_list[2], (D, KV * HD), D ** -0.5, 0.046875, ((0, 16), (1, 8)))
    v_weight = normal_values(key_list[3], (D, KV * HD), D ** -0.5, 0.046875, ((0, 16), (1, 8)))
    cache_keys = draw_cache_keys(jax.random.fold_in(key_list[8], 71), 0)
    cache_values = normal_values(key_list[5], (CACHE, KV * HD), 1.0, 6.0, ((0, 16), (1, 8)))
    cache_len = jax.random.randint(key_list[6], (1,), CACHE // 2, CACHE + 1).astype(jnp.int32)
    span_start = jax.random.randint(key_list[7], (1,), CACHE, 2 * CACHE).astype(jnp.int32)
    return {"tokens": tokens, "q_weight": q_weight, "k_weight": k_weight, "v_weight": v_weight, "cache_keys": cache_keys, "cache_values": cache_values, "cache_len": cache_len, "span_start": span_start}


def angle_table(positions, head_size):
    steps = jnp.arange(head_size // 2).astype(jnp.float32)
    freq = jnp.exp(-(2.0 * steps / head_size) * math.log(500000.0))
    return positions.astype(jnp.float32)[:, None] * freq[None, :]

def rotate(values, cos_t, sin_t, axis):
    first, second = jnp.split(values, 2, axis=axis)
    return jnp.concatenate([first * cos_t - second * sin_t, second * cos_t + first * sin_t], axis=axis)

def reference(tokens, q_weight, k_weight, v_weight, cache_keys, cache_values, cache_len, span_start):
    span = tokens.shape[0]
    group_heads = HEADS // KV
    scale = 1.0 / math.sqrt(HD)
    q_full = jnp.dot(tokens, q_weight, preferred_element_type=jnp.float32)
    k_full = jnp.dot(tokens, k_weight, preferred_element_type=jnp.float32)
    v_full = jnp.dot(tokens, v_weight, preferred_element_type=jnp.float32)
    angles = angle_table(span_start[0] + jnp.arange(span, dtype=jnp.int32), HD)
    cos_t = jnp.cos(angles)[:, None, :]
    sin_t = jnp.sin(angles)[:, None, :]
    q_rot = rotate(q_full.reshape(span, HEADS, HD), cos_t, sin_t, 2).astype(jnp.bfloat16)
    k_rot = rotate(k_full.reshape(span, KV, HD), cos_t, sin_t, 2).astype(jnp.bfloat16)
    v_rows = v_full.astype(jnp.bfloat16).reshape(span, KV, HD)
    cache_k3 = cache_keys.reshape(CACHE, KV, HD)
    cache_v3 = cache_values.reshape(CACHE, KV, HD)
    cache_seen = jnp.broadcast_to((jnp.arange(CACHE, dtype=jnp.int32) < cache_len[0])[None, :], (span, CACHE))
    index = jnp.arange(span, dtype=jnp.int32)
    block_seen = index[None, :] <= index[:, None]
    seen = jnp.concatenate([cache_seen, block_seen], axis=1)

    def one_head(head):
        group = head // group_heads
        query = lax.dynamic_index_in_dim(q_rot, head, 1, keepdims=False)
        keys = jnp.concatenate([lax.dynamic_index_in_dim(cache_k3, group, 1, keepdims=False), lax.dynamic_index_in_dim(k_rot, group, 1, keepdims=False)], axis=0)
        values = jnp.concatenate([lax.dynamic_index_in_dim(cache_v3, group, 1, keepdims=False), lax.dynamic_index_in_dim(v_rows, group, 1, keepdims=False)], axis=0)
        scores = jnp.dot(query, keys.T, preferred_element_type=jnp.float32) * scale
        top = lax.optimization_barrier(jnp.max(jnp.where(seen, scores, -1e+30), axis=1, keepdims=True))
        weights = jnp.where(seen, jnp.exp(scores - top), 0.0)
        total = lax.optimization_barrier(jnp.sum(weights, axis=1, keepdims=True))
        mixed = jnp.dot(weights.astype(jnp.bfloat16), values, preferred_element_type=jnp.float32) / total
        return mixed.astype(jnp.bfloat16)
    heads_out = lax.map(one_head, jnp.arange(HEADS, dtype=jnp.int32))
    return jnp.transpose(heads_out, (1, 0, 2)).reshape(span, HEADS * HD)
```

```python
import functools
import math

import jax
import jax.numpy as jnp
from jax import lax
from jax.experimental import pallas as pl
from jax.experimental.pallas import tpu as pltpu
from jax.sharding import PartitionSpec as P

HD = 128
NZ, NX, NC = 4, 2, 2
CHIPS = NZ * NX
SPAN = 1024
ROWS = 1024
SCALE2 = math.log2(math.e) / math.sqrt(HD)
BOOST = 64.0
NEG = -1e30


def angle_table(positions, head_size):
    steps = jnp.arange(head_size // 2).astype(jnp.float32)
    freq = jnp.exp(-(2.0 * steps / head_size) * math.log(500000.0))
    return positions.astype(jnp.float32)[:, None] * freq[None, :]


def rotate(values, cos_t, sin_t, axis):
    first, second = jnp.split(values, 2, axis=axis)
    return jnp.concatenate(
        [first * cos_t - second * sin_t, second * cos_t + first * sin_t], axis=axis
    )


def unit(z, x, c):
    return (z % NZ) * NX * NC + (x % NX) * NC + c % NC


def hop(values, dz=0, dx=0, dc=0):
    pairs = [
        (unit(z, x, c), unit(z + dz, x + dx, c + dc))
        for z in range(NZ)
        for x in range(NX)
        for c in range(NC)
    ]
    return lax.ppermute(values, "ulysses", pairs)


SAME_CORE = [[NC * p + c for p in range(CHIPS)] for c in range(NC)]


def chunk_cols(block, first, count):
    parts = [block[pl.ds(first + HD * i, HD), :] for i in range(count)]
    return jnp.concatenate(parts, axis=1)


def attention_kernel(n_blocks, meta, q_ref, new_ref, *rest):
    blocks = rest[:n_blocks]
    o_ref, held, sems = rest[n_blocks:]
    core = meta[1]
    live = meta[0]
    span = q_ref.shape[0]
    half = span // 2
    piece = half // CHIPS
    copies = []
    for i, block in enumerate(blocks):
        slot = meta[2 + i]
        copies.append(pltpu.make_async_copy(block, held.at[slot], sems.at[slot]))
    for copy in copies:
        copy.start()

    col = lax.broadcasted_iota(jnp.int32, (1, span), 1)
    own = jnp.where(col < half, core, 1 - core)
    inside = col % half
    query = (inside // piece) * (2 * piece) + own * piece + inside % piece
    q = q_ref[...]

    def scores_of(keys):
        return lax.dot_general(
            keys, q, (((1,), (1,)), ((), ())), preferred_element_type=jnp.float32
        )

    def add_values(cols, p):
        return lax.dot_general(
            cols, p.astype(jnp.bfloat16), (((1,), (0,)), ((), ())),
            preferred_element_type=jnp.float32,
        )

    def fold(p):
        return jnp.sum(p.reshape(p.shape[0] // 8, 8, p.shape[1]), axis=0)

    def wait_for(slot):
        pltpu.make_async_copy(blocks[0], held.at[slot], sems.at[slot]).wait()

    def direct(keys, cols, state, seen=None):
        acc, total = state
        p = jnp.exp2(scores_of(keys) * SCALE2)
        if seen is not None:
            p = jnp.where(seen(p.shape), p, 0.0)
        return acc + add_values(cols, p), total + fold(p)

    def causal(shape):
        return lax.broadcasted_iota(jnp.int32, shape, 0) <= query

    state = (jnp.zeros((HD, span), jnp.float32), jnp.zeros((8, span), jnp.float32))
    state = direct(new_ref[:ROWS, :], chunk_cols(new_ref, ROWS, ROWS // HD), state, causal)

    def pair(i, state):
        wait_for(2 * i)
        wait_for(2 * i + 1)
        a, b = held.at[2 * i], held.at[2 * i + 1]
        keys = jnp.concatenate([a[:ROWS, :], b[:ROWS, :]], axis=0)
        cols = jnp.concatenate(
            [chunk_cols(a, ROWS, ROWS // HD), chunk_cols(b, ROWS, ROWS // HD)], axis=1
        )
        return direct(keys, cols, state)

    def single(i, state):
        wait_for(i)
        block = held.at[i]

        def seen(shape):
            return lax.broadcasted_iota(jnp.int32, shape, 0) + i * ROWS < live

        return direct(block[:ROWS, :], chunk_cols(block, ROWS, ROWS // HD), state, seen)

    pairs = live // (2 * ROWS)
    used = (live + ROWS - 1) // ROWS
    state = lax.fori_loop(0, pairs, pair, state)
    state = lax.fori_loop(2 * pairs, used, single, state)

    def drain(i, carry):
        wait_for(i)
        return carry

    lax.fori_loop(used, n_blocks, drain, 0)
    acc, total = state
    total = jnp.sum(total, axis=0, keepdims=True)

    def write(acc, total):
        out = jnp.transpose(acc / total).astype(jnp.bfloat16)
        for part in range(2):
            place = core if part == 0 else 1 - core
            for p in range(CHIPS):
                first = part * half + p * piece
                o_ref[p, place] = out[first : first + piece, :]

    write(acc, total)
    fine = jnp.logical_and(total > 2.0**-60, total < 2.0**110)
    bad = jnp.max(jnp.where(fine, 0, 1))

    @pl.when(bad > 0)
    def _():
        def careful(keys, cols, state, seen):
            top, total, acc = state
            s = jnp.where(seen, scores_of(keys), NEG)
            new_top = jnp.maximum(top, jnp.max(s, axis=0, keepdims=True))
            factor = jnp.exp2((top - new_top) * SCALE2)
            p = jnp.where(seen, jnp.exp2((s - new_top) * SCALE2), 0.0)
            total = total * factor + jnp.sum(p, axis=0, keepdims=True)
            return new_top, total, acc * factor + add_values(cols, p)

        def step(i, state):
            block = held.at[i]
            shape = (HD * 2, span)

            def inner(j, state):
                first = pl.multiple_of(j * 2 * HD, 2 * HD)
                row = lax.broadcasted_iota(jnp.int32, shape, 0) + first
                return careful(
                    block[pl.ds(first, 2 * HD), :],
                    chunk_cols(block, ROWS + first, 2),
                    state,
                    row + i * ROWS < live,
                )

            return lax.fori_loop(0, ROWS // (2 * HD), inner, state)

        def new_step(j, state):
            first = pl.multiple_of(j * 2 * HD, 2 * HD)
            row = lax.broadcasted_iota(jnp.int32, (2 * HD, span), 0) + first
            return careful(
                new_ref[pl.ds(first, 2 * HD), :],
                chunk_cols(new_ref, ROWS + first, 2),
                state,
                row <= query,
            )

        state = (
            jnp.full((1, span), NEG, jnp.float32),
            jnp.zeros((1, span), jnp.float32),
            jnp.zeros((HD, span), jnp.float32),
        )
        state = lax.fori_loop(0, used, step, state)
        _, total, acc = lax.fori_loop(0, ROWS // (2 * HD), new_step, state)
        write(acc, total)


def attention(meta, q, new, blocks):
    n = len(blocks)
    span = q.shape[0]
    vmem = pl.BlockSpec(memory_space=pltpu.VMEM)
    return pl.pallas_call(
        functools.partial(attention_kernel, n),
        in_specs=[pl.BlockSpec(memory_space=pltpu.SMEM), vmem, vmem]
        + [pl.BlockSpec(memory_space=pl.ANY)] * n,
        out_specs=vmem,
        out_shape=jax.ShapeDtypeStruct((CHIPS, NC, span // (CHIPS * NC), HD), jnp.bfloat16),
        scratch_shapes=[
            pltpu.VMEM((n, 2 * ROWS, HD), jnp.bfloat16),
            pltpu.SemaphoreType.DMA((n,)),
        ],
        compiler_params=pltpu.CompilerParams(vmem_limit_bytes=48 * 2**20),
        cost_estimate=pl.CostEstimate(
            flops=4 * span * HD * ROWS * (n + 1),
            bytes_accessed=2 * n * 2 * ROWS * HD,
            transcendentals=span * ROWS * (n + 1),
        ),
    )(meta, q, new, *blocks)


def on_device(
    tokens, q_weight, k_weight, v_weight, cache_keys, cache_values, cache_len, span_start
):
    n_tensor = lax.axis_size("tensor")
    me = lax.axis_index("ulysses")
    core = me % NC
    chip = me // NC
    own_rows = tokens.shape[0]
    width = q_weight.shape[1] // NC
    depth = q_weight.shape[0]

    mine = lax.all_to_all(
        tokens.reshape(own_rows, CHIPS, NC * depth),
        "ulysses",
        split_axis=1,
        concat_axis=0,
        axis_index_groups=SAME_CORE,
        tiled=True,
    ).reshape(CHIPS * own_rows, NC * depth)

    both = jnp.stack([k_weight, v_weight])
    keep = jnp.concatenate(
        [
            lax.dynamic_slice_in_dim(q_weight, core * width, width, 1),
            lax.dynamic_index_in_dim(both, core, 0, keepdims=False),
        ],
        axis=1,
    )
    give = jnp.concatenate(
        [
            lax.dynamic_slice_in_dim(q_weight, (1 - core) * width, width, 1),
            lax.dynamic_index_in_dim(both, 1 - core, 0, keepdims=False),
        ],
        axis=1,
    )
    got = hop(give, dc=1)
    weight = jnp.where(
        core == 0,
        jnp.concatenate([keep, got], axis=0),
        jnp.concatenate([got, keep], axis=0),
    )

    cols = jnp.transpose(cache_values.reshape(ROWS // HD, HD, HD), (0, 2, 1)).reshape(ROWS, HD)
    b000 = jnp.concatenate([cache_keys, cols], axis=0)
    b300 = hop(b000, dz=1)
    b100 = hop(b000, dz=-1)
    b010 = hop(b000, dx=1)
    b310 = hop(b010, dz=1)
    b200 = hop(b100, dz=-1)
    b110 = hop(b100, dx=1)
    b210 = hop(b200, dx=1)
    lineage = {
        (0, 0): b000, (1, 0): b100, (2, 0): b200, (3, 0): b300,
        (0, 1): b010, (1, 1): b110, (2, 1): b210, (3, 1): b310,
    }
    blocks, slots = [], []
    z_me, x_me = chip // NX, chip % NX
    for (dz, dx), block in lineage.items():
        place = ((z_me + dz) % NZ) * NX * NC + ((x_me + dx) % NX) * NC
        blocks += [block, hop(block, dc=1)]
        slots += [place + core, place + 1 - core]

    other = hop(mine, dc=1)
    spread = jnp.concatenate([mine, other], axis=0)
    span = spread.shape[0]
    heads = width // HD

    kv_part = jnp.dot(spread, weight[:, width:], preferred_element_type=jnp.float32)
    kv_parts = lax.all_to_all(
        kv_part.reshape(NC, CHIPS, own_rows, HD),
        "ulysses",
        split_axis=1,
        concat_axis=1,
        axis_index_groups=SAME_CORE,
        tiled=True,
    )
    kv_sum = jnp.sum(kv_parts, axis=1)
    kv_sum = jnp.where(core == 0, kv_sum, kv_sum[::-1]).reshape(NC * own_rows, HD)
    kv_pos = span_start[0] + chip * NC * own_rows + jnp.arange(NC * own_rows, dtype=jnp.int32)
    kv_angles = angle_table(kv_pos, HD)
    k_rot = rotate(kv_sum, jnp.cos(kv_angles), jnp.sin(kv_angles), 1)
    kv_own = jnp.where(core == 0, k_rot, kv_sum.T).astype(jnp.bfloat16)
    kv_all = lax.all_to_all(
        jnp.broadcast_to(kv_own[None], (CHIPS,) + kv_own.shape),
        "ulysses",
        split_axis=0,
        concat_axis=0,
        axis_index_groups=SAME_CORE,
        tiled=True,
    ).reshape(SPAN, HD)
    kv_other = hop(kv_all, dc=1)
    new = jnp.where(
        core == 0,
        jnp.concatenate([kv_all, kv_other], axis=0),
        jnp.concatenate([kv_other, kv_all], axis=0),
    )

    q_part = jnp.einsum(
        "td,dhk->htk",
        spread,
        weight[:, :width].reshape(NC * depth, heads, HD),
        preferred_element_type=jnp.float32,
    )
    q_parts = lax.all_to_all(
        (q_part * BOOST).astype(jnp.float16),
        "ulysses",
        split_axis=0,
        concat_axis=0,
        axis_index_groups=SAME_CORE,
        tiled=True,
    )
    q_sum = jnp.sum(q_parts.astype(jnp.float32), axis=0) * (1.0 / BOOST)
    row = jnp.arange(span, dtype=jnp.int32)
    half = span // 2
    own = jnp.where(row < half, core, 1 - core)
    inside = row % half
    index = (inside // own_rows) * NC * own_rows + own * own_rows + inside % own_rows
    angles = angle_table(span_start[0] + index, HD)
    q_rot = rotate(q_sum, jnp.cos(angles), jnp.sin(angles), 1).astype(jnp.bfloat16)

    meta = jnp.stack([cache_len[0], core] + slots).astype(jnp.int32)
    mixed = attention(meta, q_rot, new, blocks).reshape(span, HD)
    n_all = n_tensor * NC * CHIPS
    moved = lax.all_to_all(
        mixed.reshape(n_all, span // n_all, HD),
        ("tensor", "ulysses"),
        split_axis=0,
        concat_axis=0,
        tiled=True,
    )
    moved = moved.reshape(n_tensor, CHIPS, NC, span // n_all, HD)
    return jnp.transpose(moved, (3, 0, 2, 1, 4)).reshape(span // n_all, n_all * HD)


def solution(mesh):
    placed = (
        P("ulysses", None),
        P("ulysses", "tensor"),
        P("ulysses", "tensor"),
        P("ulysses", "tensor"),
        P("ulysses", "tensor"),
        P("ulysses", "tensor"),
        P(),
        P(),
    )
    return jax.shard_map(
        on_device,
        mesh=mesh,
        in_specs=placed,
        out_specs=P(("tensor", "ulysses"), None),
        check_vma=False,
    )
```

```python
import functools
import math

import jax
import jax.numpy as jnp
from jax import lax
from jax.experimental import pallas as pl
from jax.experimental.pallas import tpu as pltpu
from jax.sharding import PartitionSpec as P

HD = 128
NZ, NX, NC = 4, 2, 2
CHIPS = NZ * NX
NY = 4
META = 3
SPAN = 1024
ROWS = 1024
SCALE2 = math.log2(math.e) / math.sqrt(HD)
BOOST = 64.0
LOW = 2048.0
NEG = -1e30


def angle_table(positions, head_size):
    steps = jnp.arange(head_size // 2).astype(jnp.float32)
    freq = jnp.exp(-(2.0 * steps / head_size) * math.log(500000.0))
    return positions.astype(jnp.float32)[:, None] * freq[None, :]


def rotate(values, cos_t, sin_t, axis):
    first, second = jnp.split(values, 2, axis=axis)
    return jnp.concatenate(
        [first * cos_t - second * sin_t, second * cos_t + first * sin_t], axis=axis
    )


def unit(z, x, c):
    return (z % NZ) * NX * NC + (x % NX) * NC + c % NC


def hop(values, dz=0, dx=0, dc=0):
    pairs = [
        (unit(z, x, c), unit(z + dz, x + dx, c + dc))
        for z in range(NZ)
        for x in range(NX)
        for c in range(NC)
    ]
    return lax.ppermute(values, "ulysses", pairs)


def hop_y(values, dy):
    pairs = [(x * NY + y, x * NY + (y + dy) % NY) for x in range(2) for y in range(NY)]
    return lax.ppermute(values, "tensor", pairs)


SAME_CORE = [[NC * p + c for p in range(CHIPS)] for c in range(NC)]


def chunk_cols(block, first, count):
    parts = [block[pl.ds(first + HD * i, HD), :] for i in range(count)]
    return jnp.concatenate(parts, axis=1)


def trans_dot(keys, q):
    return lax.dot_general(keys, q, (((1,), (1,)), ((), ())), preferred_element_type=jnp.float32)


def add_values(cols, p):
    return lax.dot_general(
        cols, p.astype(jnp.bfloat16), (((1,), (0,)), ((), ())), preferred_element_type=jnp.float32
    )


def direct(q, keys, cols, state, seen=None):
    acc, total = state
    p = jnp.exp2(trans_dot(keys, q) * SCALE2)
    if seen is not None:
        p = jnp.where(seen(p.shape), p, 0.0)
    folded = jnp.sum(p.reshape(p.shape[0] // 8, 8, p.shape[1]), axis=0)
    return acc + add_values(cols, p), total + folded


def load_cache(pieces, places, meta, held, sems):
    for ref, (slot, first) in zip(pieces, places):
        place = meta[META + slot]
        rows = ref.shape[0]
        pltpu.make_async_copy(ref, held.at[place, pl.ds(first, rows)], sems.at[place]).start()


def turned(q_ref, cos_ref, sin_ref):
    raw = q_ref[...]
    turned_q = raw * cos_ref[...] + pltpu.roll(raw, HD // 2, 1) * sin_ref[...]
    return turned_q.astype(jnp.bfloat16)


def over_cache(q, live, held, sems, state):
    def wait_for(slot):
        pltpu.make_async_copy(held.at[slot], held.at[slot], sems.at[slot]).wait()

    def pair(i, state):
        wait_for(2 * i)
        wait_for(2 * i + 1)
        a, b = held.at[2 * i], held.at[2 * i + 1]
        keys = jnp.concatenate([a[:ROWS, :], b[:ROWS, :]], axis=0)
        cols = jnp.concatenate(
            [chunk_cols(a, ROWS, ROWS // HD), chunk_cols(b, ROWS, ROWS // HD)], axis=1
        )
        return direct(q, keys, cols, state)

    def single(i, state):
        wait_for(i)
        block = held.at[i]

        def seen(shape):
            return lax.broadcasted_iota(jnp.int32, shape, 0) + i * ROWS < live

        return direct(q, block[:ROWS, :], chunk_cols(block, ROWS, ROWS // HD), state, seen)

    def drain(i, carry):
        wait_for(i)
        return carry

    pairs = live // (2 * ROWS)
    used = (live + ROWS - 1) // ROWS
    state = lax.fori_loop(0, pairs, pair, state)
    state = lax.fori_loop(2 * pairs, used, single, state)
    lax.fori_loop(used, held.shape[0], drain, 0)
    return state


def empty_state(span):
    return jnp.zeros((HD, span), jnp.float32), jnp.zeros((8, span), jnp.float32)


def first_kernel(places, meta, q_ref, cos_ref, sin_ref, *rest):
    pieces = rest[: len(places)]
    acc_ref, total_ref, turned_ref, held, sems = rest[len(places) :]
    load_cache(pieces, places, meta, held, sems)
    q = turned(q_ref, cos_ref, sin_ref)
    turned_ref[...] = q
    acc, total = over_cache(q, meta[0], held, sems, empty_state(q.shape[0]))
    acc_ref[...] = acc
    total_ref[...] = total


def last_kernel(places, meta, acc_a, total_a, turned_a, acc_b, total_b, turned_b, new_ref, *rest):
    pieces = rest[: len(places)]
    o_ref, held, sems = rest[len(places) :]
    live, core, parity = meta[0], meta[1], meta[2]
    span = turned_a.shape[0]
    part = span // NC
    piece = part // CHIPS

    col = lax.broadcasted_iota(jnp.int32, (1, span), 1)
    kind = jnp.where(col < part, core, 1 - core)
    inside = col % part
    base = (inside // piece) * (4 * piece) + kind * (2 * piece) + inside % piece
    query_a, query_b = base + parity * piece, base + (1 - parity) * piece

    def before(query):
        return lambda shape: lax.broadcasted_iota(jnp.int32, shape, 0) <= query

    new_keys = jnp.concatenate([new_ref[NC * p] for p in range(CHIPS)], axis=0)
    new_cols = jnp.concatenate([new_ref[NC * p + 1] for p in range(CHIPS)], axis=1)
    q_a = turned_a[...]
    state_a = direct(q_a, new_keys, new_cols, (acc_a[...], total_a[...]), before(query_a))
    q_b = turned_b[...]
    state_b = direct(q_b, new_keys, new_cols, (acc_b[...], total_b[...]), before(query_b))

    def write(acc, total, sub):
        out = jnp.transpose(acc / total).astype(jnp.bfloat16)
        for k in range(NC):
            place = core if k == 0 else 1 - core
            for p in range(CHIPS):
                first = k * part + p * piece
                o_ref[p, place, sub] = out[first : first + piece, :]

    def is_bad(total):
        fine = jnp.logical_and(total > 2.0**-60, total < 2.0**110)
        return jnp.max(jnp.where(fine, 0, 1))

    def finish(state, sub):
        acc, total = state
        total = jnp.sum(total, axis=0, keepdims=True)
        write(acc, total, sub)
        return is_bad(total)

    def recompute(q, query, sub):
        def careful(keys, cols, state, seen):
            top, total, acc = state
            s = jnp.where(seen, trans_dot(keys, q), NEG)
            new_top = jnp.maximum(top, jnp.max(s, axis=0, keepdims=True))
            factor = jnp.exp2((top - new_top) * SCALE2)
            p = jnp.where(seen, jnp.exp2((s - new_top) * SCALE2), 0.0)
            total = total * factor + jnp.sum(p, axis=0, keepdims=True)
            return new_top, total, acc * factor + add_values(cols, p)

        def rows_from(first):
            return lax.broadcasted_iota(jnp.int32, (2 * HD, span), 0) + first

        def step(i, state):
            block = held.at[i]

            def inner(j, state):
                first = pl.multiple_of(j * 2 * HD, 2 * HD)
                keys = block[pl.ds(first, 2 * HD), :]
                cols = chunk_cols(block, ROWS + first, 2)
                return careful(keys, cols, state, rows_from(first) + i * ROWS < live)

            return lax.fori_loop(0, ROWS // (2 * HD), inner, state)

        def new_step(j, state):
            first = 2 * NC * j
            keys = jnp.concatenate([new_ref[first], new_ref[first + NC]], axis=0)
            cols = jnp.concatenate([new_ref[first + 1], new_ref[first + NC + 1]], axis=1)
            return careful(keys, cols, state, rows_from(j * 2 * HD) <= query)

        state = (
            jnp.full((1, span), NEG, jnp.float32),
            jnp.zeros((1, span), jnp.float32),
            jnp.zeros((HD, span), jnp.float32),
        )
        state = lax.fori_loop(0, (live + ROWS - 1) // ROWS, step, state)
        _, total, acc = lax.fori_loop(0, ROWS // (2 * HD), new_step, state)
        write(acc, total, sub)

    bad = jnp.maximum(finish(state_a, parity), finish(state_b, 1 - parity))

    @pl.when(bad > 0)
    def _():
        load_cache(pieces, places, meta, held, sems)

        def drain(i, carry):
            pltpu.make_async_copy(held.at[i], held.at[i], sems.at[i]).wait()
            return carry

        lax.fori_loop(0, held.shape[0], drain, 0)
        recompute(q_a, query_a, parity)
        recompute(q_b, query_b, 1 - parity)


def attention_call(kernel, meta, arrays, pieces, places, out_shape):
    span = SPAN // 2
    n = NC * CHIPS
    vmem = pl.BlockSpec(memory_space=pltpu.VMEM)
    return pl.pallas_call(
        functools.partial(kernel, places),
        in_specs=[pl.BlockSpec(memory_space=pltpu.SMEM)]
        + [vmem] * len(arrays)
        + [pl.BlockSpec(memory_space=pl.ANY)] * len(pieces),
        out_specs=jax.tree.map(lambda _: vmem, out_shape),
        out_shape=out_shape,
        scratch_shapes=[
            pltpu.VMEM((n, 2 * ROWS, HD), jnp.bfloat16),
            pltpu.SemaphoreType.DMA((n,)),
        ],
        compiler_params=pltpu.CompilerParams(vmem_limit_bytes=60 * 2**20),
        cost_estimate=pl.CostEstimate(
            flops=4 * span * HD * ROWS * (n + 1),
            bytes_accessed=2 * n * 2 * ROWS * HD,
            transcendentals=span * ROWS * (n + 1),
        ),
    )(meta, *arrays, *pieces)


def project_kernel(n_parts, meta, *rest):
    parts = rest[:n_parts]
    w_own, w_got, k_own, v_own, kv_got, o_ref, x_ref, kv_ref = rest[n_parts:]
    depth = w_own.shape[0]
    core = meta[0]
    own = pl.ds(pl.multiple_of(core * depth, depth), depth)
    got = pl.ds(pl.multiple_of((1 - core) * depth, depth), depth)

    def times(own_cols, got_cols):
        out = jnp.dot(x_ref[:, own], own_cols, preferred_element_type=jnp.float32)
        out += jnp.dot(x_ref[:, got], got_cols, preferred_element_type=jnp.float32)
        return out * BOOST

    @pl.when(pl.program_id(0) == 0)
    def _():
        first = 0
        for part in parts:
            x_ref[pl.ds(first, part.shape[0]), :] = part[...]
            first += part.shape[0]
        kv_ref[...] = times(jnp.where(core == 0, k_own[...], v_own[...]), kv_got[...])

    out = times(w_own[...], w_got[...])
    heads, span = o_ref.shape[0], x_ref.shape[0]
    kind = span // NC
    few = kind // CHIPS
    for h in range(heads):
        o_ref[h, :span, :] = out[:, h * HD : (h + 1) * HD]
        chip = pl.program_id(0) * heads + h
        for k in range(NC):
            value = kv_ref[pl.ds(pl.multiple_of(k * kind + chip * few, few), few), :]
            wide = value * 8193.0
            high = wide - (wide - value)
            high = jnp.where(jnp.abs(value) < 2.0**-14, 0.0, high)
            o_ref[h, pl.ds(span + k * few, few), :] = high
            o_ref[h, pl.ds(span + (NC + k) * few, few), :] = (value - high) * LOW


def project(core, parts, q_weight, k_weight, v_weight, got):
    depth, width = q_weight.shape[0], q_weight.shape[1] // NC
    span = sum(part.shape[0] for part in parts)
    tile = 2 * HD
    steps = width // tile
    rows = span + 2 * span // CHIPS
    whole = lambda n, m: (0, 0)
    return pl.pallas_call(
        functools.partial(project_kernel, len(parts)),
        grid_spec=pltpu.PrefetchScalarGridSpec(
            num_scalar_prefetch=1,
            grid=(steps,),
            in_specs=[pl.BlockSpec(part.shape, whole) for part in parts]
            + [
                pl.BlockSpec((depth, tile), lambda n, m: (0, m[0] * steps + n)),
                pl.BlockSpec((depth, tile), lambda n, m: (0, n)),
                pl.BlockSpec((depth, HD), whole),
                pl.BlockSpec((depth, HD), whole),
                pl.BlockSpec((depth, HD), whole),
            ],
            out_specs=pl.BlockSpec((tile // HD, rows, HD), lambda n, m: (n, 0, 0)),
            scratch_shapes=[
                pltpu.VMEM((span, NC * depth), jnp.bfloat16),
                pltpu.VMEM((span, HD), jnp.float32),
            ],
        ),
        out_shape=jax.ShapeDtypeStruct((width // HD, rows, HD), jnp.float32),
        compiler_params=pltpu.CompilerParams(vmem_limit_bytes=24 * 2**20),
        cost_estimate=pl.CostEstimate(
            flops=4 * span * depth * width,
            bytes_accessed=4 * span * depth + 4 * depth * width + 4 * span * width,
            transcendentals=0,
        ),
    )(core[None], *parts, q_weight, got[0], k_weight, v_weight, got[1])


def settle_kernel(meta, kv_a, kv_b, cos_ref, sin_ref, o_ref, rows):
    core, parity = meta[0], meta[1]
    few = kv_a.shape[1]
    for sub, kv in ((parity, kv_a), (1 - parity, kv_b)):
        for k, kind in enumerate((core, 1 - core)):
            first = pl.multiple_of((2 * kind + sub) * few, few)
            rows[pl.ds(first, few), :] = kv[k]
    value = rows[...]
    key = value * cos_ref[...] + pltpu.roll(value, HD // 2, 1) * sin_ref[...]
    out = jnp.where(core == 0, key, jnp.transpose(value)).astype(jnp.bfloat16)
    for i in range(o_ref.shape[0]):
        o_ref[i] = out


def settle(core, parity, kv_a, kv_b, cos_t, sin_t):
    vmem = pl.BlockSpec(memory_space=pltpu.VMEM)
    return pl.pallas_call(
        settle_kernel,
        in_specs=[pl.BlockSpec(memory_space=pltpu.SMEM)] + [vmem] * 4,
        out_specs=vmem,
        out_shape=jax.ShapeDtypeStruct((NC * CHIPS, HD, HD), jnp.bfloat16),
        scratch_shapes=[pltpu.VMEM((HD, HD), jnp.float32)],
    )(jnp.stack([core, parity]), kv_a, kv_b, cos_t, sin_t)


def tables(positions):
    angles = angle_table(positions, HD)
    cos_t, sin_t = jnp.cos(angles), jnp.sin(angles)
    return jnp.concatenate([cos_t, cos_t], axis=1), jnp.concatenate([-sin_t, sin_t], axis=1)


def trade(values, axis):
    return lax.all_to_all(
        values,
        "ulysses",
        split_axis=axis,
        concat_axis=axis,
        axis_index_groups=SAME_CORE,
        tiled=True,
    )


def on_device(
    tokens, q_weight, k_weight, v_weight, cache_keys, cache_values, cache_len, span_start
):
    barrier = lax.optimization_barrier
    n_tensor = lax.axis_size("tensor")
    me = lax.axis_index("ulysses").astype(jnp.int32)
    core = me % NC
    chip = me // NC
    parity = lax.axis_index("tensor").astype(jnp.int32) % 2
    own_rows, features = tokens.shape
    few = own_rows // 2
    depth, width = q_weight.shape[0], q_weight.shape[1] // NC

    cols = jnp.transpose(cache_values.reshape(ROWS // HD, HD, HD), (0, 2, 1)).reshape(ROWS, HD)
    b000 = jnp.concatenate([cache_keys, cols], axis=0)
    b300 = hop(b000, dz=1)
    b100 = hop(b000, dz=-1)
    b010 = hop(b000, dx=1)

    part = lax.dynamic_slice_in_dim(tokens, parity * few, few, 0)
    mine = trade(
        jnp.transpose(part.reshape(few, CHIPS, NC * depth), (1, 0, 2)), 0
    ).reshape(CHIPS * few, NC * depth)

    near = jnp.arange(few, dtype=jnp.int32)[None, None, :]
    kinds = jnp.stack([core, 1 - core])[:, None, None]
    of_chip = jnp.arange(CHIPS, dtype=jnp.int32)[None, :, None]
    index = (of_chip * 4 * few + kinds * 2 * few + near).reshape(-1) + span_start[0]
    turn_a = tables(index + parity * few)
    turn_b = tables(index + (1 - parity) * few)
    turn_kv = tables(
        span_start[0] + chip * 4 * few + jnp.arange(4 * few, dtype=jnp.int32)
    )

    q_got = hop(lax.dynamic_slice_in_dim(q_weight, (1 - core) * width, width, 1), dc=1)
    kv_got = hop(jnp.where(core == 0, v_weight, k_weight), dc=1)
    got = (q_got, kv_got)

    mine, got, b300, b100, b010, turn_a, turn_b, turn_kv = barrier(
        (mine, got, b300, b100, b010, turn_a, turn_b, turn_kv)
    )
    far = CHIPS * few // 2
    other = [hop_y(mine[:far], 1), hop_y(mine[far:], -1)]
    mine_twin = hop(mine, dc=1)

    def sums(parts):
        return project(core, parts, q_weight, k_weight, v_weight, got).astype(jnp.float16)

    half = SPAN // 2

    def total_of(parts):
        return jnp.sum(parts[:, :half].astype(jnp.float32), axis=0) * (1.0 / BOOST)

    def kv_of(parts):
        rows = jnp.sum(parts[:, half:].astype(jnp.float32), axis=0).reshape(2, NC, few, HD)
        return (rows[0] + rows[1] * (1.0 / LOW)) * (1.0 / BOOST)

    b310 = hop(b010, dz=1)
    b200 = hop(b100, dz=-1)
    b110 = hop(b100, dx=1)
    first_own = [b000, b300, b100, b010]

    sent_a = trade(sums([mine, mine_twin]), 0)
    other, b310, b200, b110 = barrier((other, b310, b200, b110))
    other_twin = [hop(x, dc=1) for x in other]
    first_swap = [hop(b, dc=1) for b in first_own]
    q_b = sums(other + other_twin)
    b210k = hop(b200[:ROWS], dx=1)
    b210v = hop(b310[ROWS:], dz=1)
    q_b, first_swap, b210k, b210v = barrier((q_b, first_swap, b210k, b210v))
    sent_b = trade(q_b, 0)
    second_own = [b310, b200, b110]
    second_swap = [hop(b, dc=1) for b in second_own]

    z_me, x_me = chip // NX, chip % NX
    pieces, places, slots = [], [], []

    def add(own, swap, dz, dx, first=0, fresh=True):
        if fresh:
            place = ((z_me + dz) % NZ) * NX * NC + ((x_me + dx) % NX) * NC
            slots.extend([place + core, place + 1 - core])
        pieces.extend([own, swap])
        places.extend([(len(slots) - 2, first), (len(slots) - 1, first)])

    for own, swap, (dz, dx) in zip(
        first_own + second_own,
        first_swap + second_swap,
        [(0, 0), (3, 0), (1, 0), (0, 1), (3, 1), (2, 0), (1, 1)],
    ):
        add(own, swap, dz, dx)
    add(b210k, hop(b210k, dc=1), 2, 1)
    add(b210v, hop(b210v, dc=1), 2, 1, ROWS, False)
    places = tuple(places)
    meta = jnp.stack([cache_len[0], core, parity] + slots).astype(jnp.int32)

    def attend(sent, turn):
        return attention_call(
            first_kernel,
            meta,
            [total_of(sent), *turn],
            pieces,
            places,
            (
                jax.ShapeDtypeStruct((HD, half), jnp.float32),
                jax.ShapeDtypeStruct((8, half), jnp.float32),
                jax.ShapeDtypeStruct((half, HD), jnp.bfloat16),
            ),
        )

    state_a = attend(sent_a, turn_a)
    sent_b, state_a = barrier((sent_b, state_a))
    state_b = attend(sent_b, turn_b)

    settled = settle(core, parity, kv_of(sent_a), kv_of(sent_b), *turn_kv)
    new = lax.all_to_all(settled, "ulysses", split_axis=0, concat_axis=0, tiled=True)
    new, state_b = barrier((new, state_b))
    mixed = attention_call(
        last_kernel,
        meta,
        [*state_a, *state_b, new],
        pieces,
        places,
        jax.ShapeDtypeStruct((CHIPS, NC, 2, few, HD), jnp.bfloat16),
    )
    n_all = n_tensor * NC * CHIPS
    out_rows = SPAN // n_all
    moved = lax.all_to_all(
        mixed.reshape(n_all, out_rows, HD),
        ("tensor", "ulysses"),
        split_axis=0,
        concat_axis=0,
        tiled=True,
    )
    moved = moved.reshape(n_tensor, CHIPS, NC, out_rows, HD)
    return jnp.transpose(moved, (3, 0, 2, 1, 4)).reshape(out_rows, n_all * HD)


def solution(mesh):
    placed = (
        P("ulysses", None),
        P("ulysses", "tensor"),
        P("ulysses", "tensor"),
        P("ulysses", "tensor"),
        P("ulysses", "tensor"),
        P("ulysses", "tensor"),
        P(),
        P(),
    )
    return jax.shard_map(
        on_device,
        mesh=mesh,
        in_specs=placed,
        out_specs=P(("tensor", "ulysses"), None),
        check_vma=False,
    )
```

```python
import functools
import math

import jax
import jax.numpy as jnp
from jax import lax
from jax.experimental import pallas as pl
from jax.experimental.pallas import tpu as pltpu
from jax.sharding import PartitionSpec as P

HD = 128
NZ, NX, NC = 4, 2, 2
CHIPS = NZ * NX
NY = 4
META = 5
SPAN = 1024
ROWS = 1024
SCALE2 = math.log2(math.e) / math.sqrt(HD)
BOOST = 64.0
LOW = 2048.0
NEG = -1e30


def angle_table(positions, head_size):
    steps = jnp.arange(head_size // 2).astype(jnp.float32)
    freq = jnp.exp(-(2.0 * steps / head_size) * math.log(500000.0))
    return positions.astype(jnp.float32)[:, None] * freq[None, :]


def rotate(values, cos_t, sin_t, axis):
    first, second = jnp.split(values, 2, axis=axis)
    return jnp.concatenate(
        [first * cos_t - second * sin_t, second * cos_t + first * sin_t], axis=axis
    )


def unit(z, x, c):
    return (z % NZ) * NX * NC + (x % NX) * NC + c % NC


def hop(values, dz=0, dx=0, dc=0):
    pairs = [
        (unit(z, x, c), unit(z + dz, x + dx, c + dc))
        for z in range(NZ)
        for x in range(NX)
        for c in range(NC)
    ]
    return lax.ppermute(values, "ulysses", pairs)


def hop_y(values, dy):
    pairs = [(x * NY + y, x * NY + (y + dy) % NY) for x in range(2) for y in range(NY)]
    return lax.ppermute(values, "tensor", pairs)


SAME_CORE = [[NC * p + c for p in range(CHIPS)] for c in range(NC)]


def chunk_cols(block, first, count):
    parts = [block[pl.ds(first + HD * i, HD), :] for i in range(count)]
    return jnp.concatenate(parts, axis=1)


def trans_dot(keys, q):
    return lax.dot_general(keys, q, (((1,), (1,)), ((), ())), preferred_element_type=jnp.float32)


def add_values(cols, p):
    return lax.dot_general(
        cols, p.astype(jnp.bfloat16), (((1,), (0,)), ((), ())), preferred_element_type=jnp.float32
    )


def direct(q, keys, cols, state, seen=None):
    acc, total = state
    p = jnp.exp2(trans_dot(keys, q) * SCALE2)
    if seen is not None:
        p = jnp.where(seen(p.shape), p, 0.0)
    folded = jnp.sum(p.reshape(p.shape[0] // 8, 8, p.shape[1]), axis=0)
    return acc + add_values(cols, p), total + folded


def load_cache(pieces, places, meta, held, sems):
    live, z_me = meta[0], meta[3]

    def load(ref, slot, first):
        place = meta[META + slot]

        @pl.when(place * ROWS < live)
        def _():
            rows = pl.ds(first, ref.shape[0])
            pltpu.make_async_copy(ref, held.at[place, rows], sems.at[place]).start()

    for z in range(NZ):

        @pl.when(z_me == z)
        def _(z=z):
            order = sorted(range(len(places)), key=lambda i: (z + places[i][2]) % NZ)
            for i in order:
                load(pieces[i], *places[i][:2])


def turned(q_ref, cos_ref, sin_ref):
    raw = q_ref[: cos_ref.shape[0], :] * (1.0 / BOOST)
    turned_q = raw * cos_ref[...] + pltpu.roll(raw, HD // 2, 1) * sin_ref[...]
    return turned_q.astype(jnp.bfloat16)


def one_block(q, i, live, held, state):
    block = held.at[i]

    def seen(shape):
        return lax.broadcasted_iota(jnp.int32, shape, 0) + i * ROWS < live

    return direct(q, block[:ROWS, :], chunk_cols(block, ROWS, ROWS // HD), state, seen)


def over_cache(q, live, held, sems, state, skip=None):
    def wait_for(slot):
        pltpu.make_async_copy(held.at[slot], held.at[slot], sems.at[slot]).wait()

    def pair(i, state):
        wait_for(2 * i)
        wait_for(2 * i + 1)
        a, b = held.at[2 * i], held.at[2 * i + 1]
        keys = jnp.concatenate([a[:ROWS, :], b[:ROWS, :]], axis=0)
        cols = jnp.concatenate(
            [chunk_cols(a, ROWS, ROWS // HD), chunk_cols(b, ROWS, ROWS // HD)], axis=1
        )
        return direct(q, keys, cols, state)

    def single(i, state):
        wait_for(i)
        return one_block(q, i, live, held, state)

    pairs = live // (2 * ROWS)
    used = (live + ROWS - 1) // ROWS
    if skip is None:
        state = lax.fori_loop(0, pairs, pair, state)
        return lax.fori_loop(2 * pairs, used, single, state)
    count = pairs - jnp.where(skip < pairs, 1, 0)
    state = lax.fori_loop(0, count, lambda i, s: pair(i + jnp.where(i >= skip, 1, 0), s), state)
    end = jnp.where(skip == pairs, 2 * pairs, used)
    return lax.fori_loop(2 * pairs, end, single, state)


def empty_state(span):
    return jnp.zeros((HD, span), jnp.float32), jnp.zeros((8, span), jnp.float32)


def first_kernel(places, meta, q_ref, cos_ref, sin_ref, *rest):
    pieces = rest[: len(places)]
    acc_ref, total_ref, turned_ref, held, sems = rest[len(places) :]
    load_cache(pieces, places, meta, held, sems)
    q = turned(q_ref, cos_ref, sin_ref)
    turned_ref[...] = q
    start = empty_state(q.shape[0])
    acc, total = over_cache(q, meta[0], held, sems, start, skip=meta[4])
    acc_ref[...] = acc
    total_ref[...] = total


def second_kernel(places, meta, q_ref, cos_ref, sin_ref, acc_a, total_a, turned_a, *rest):
    pieces = rest[: len(places)]
    acc_ref, total_ref, turned_ref, acc_out, total_out, held, sems = rest[len(places) :]
    load_cache(pieces, places, meta, held, sems)
    q = turned(q_ref, cos_ref, sin_ref)
    turned_ref[...] = q
    live, late = meta[0], 2 * meta[4]
    acc, total = over_cache(q, live, held, sems, empty_state(q.shape[0]))
    acc_ref[...] = acc
    total_ref[...] = total
    q_a = turned_a[...]
    end = jnp.clip((live + ROWS - 1) // ROWS, late, late + 2)
    acc, total = lax.fori_loop(
        late, end, lambda i, s: one_block(q_a, i, live, held, s), (acc_a[...], total_a[...])
    )
    acc_out[...] = acc
    total_out[...] = total


def last_kernel(places, meta, acc_a, total_a, turned_a, acc_b, total_b, turned_b, new_ref, *rest):
    pieces = rest[: len(places)]
    o_ref, held, sems = rest[len(places) :]
    live, core, parity = meta[0], meta[1], meta[2]
    span = turned_a.shape[0]
    part = span // NC
    piece = part // CHIPS

    col = lax.broadcasted_iota(jnp.int32, (1, span), 1)
    kind = jnp.where(col < part, core, 1 - core)
    inside = col % part
    base = (inside // piece) * (4 * piece) + kind * (2 * piece) + inside % piece
    query_a, query_b = base + parity * piece, base + (1 - parity) * piece

    def before(query):
        return lambda shape: lax.broadcasted_iota(jnp.int32, shape, 0) <= query

    new_keys = jnp.concatenate([new_ref[NC * p] for p in range(CHIPS)], axis=0)
    new_cols = jnp.concatenate([new_ref[NC * p + 1] for p in range(CHIPS)], axis=1)
    q_a = turned_a[...]
    state_a = direct(q_a, new_keys, new_cols, (acc_a[...], total_a[...]), before(query_a))
    q_b = turned_b[...]
    state_b = direct(q_b, new_keys, new_cols, (acc_b[...], total_b[...]), before(query_b))

    def write(acc, total, sub):
        out = jnp.transpose(acc / total).astype(jnp.bfloat16)
        for k in range(NC):
            place = core if k == 0 else 1 - core
            for p in range(CHIPS):
                first = k * part + p * piece
                o_ref[p, place, sub] = out[first : first + piece, :]

    def is_bad(total):
        fine = jnp.logical_and(total > 2.0**-60, total < 2.0**110)
        return jnp.max(jnp.where(fine, 0, 1))

    def finish(state, sub):
        acc, total = state
        total = jnp.sum(total, axis=0, keepdims=True)
        write(acc, total, sub)
        return is_bad(total)

    def recompute(q, query, sub):
        def careful(keys, cols, state, seen):
            top, total, acc = state
            s = jnp.where(seen, trans_dot(keys, q), NEG)
            new_top = jnp.maximum(top, jnp.max(s, axis=0, keepdims=True))
            factor = jnp.exp2((top - new_top) * SCALE2)
            p = jnp.where(seen, jnp.exp2((s - new_top) * SCALE2), 0.0)
            total = total * factor + jnp.sum(p, axis=0, keepdims=True)
            return new_top, total, acc * factor + add_values(cols, p)

        def rows_from(first):
            return lax.broadcasted_iota(jnp.int32, (2 * HD, span), 0) + first

        def step(i, state):
            block = held.at[i]

            def inner(j, state):
                first = pl.multiple_of(j * 2 * HD, 2 * HD)
                keys = block[pl.ds(first, 2 * HD), :]
                cols = chunk_cols(block, ROWS + first, 2)
                return careful(keys, cols, state, rows_from(first) + i * ROWS < live)

            return lax.fori_loop(0, ROWS // (2 * HD), inner, state)

        def new_step(j, state):
            first = 2 * NC * j
            keys = jnp.concatenate([new_ref[first], new_ref[first + NC]], axis=0)
            cols = jnp.concatenate([new_ref[first + 1], new_ref[first + NC + 1]], axis=1)
            return careful(keys, cols, state, rows_from(j * 2 * HD) <= query)

        state = (
            jnp.full((1, span), NEG, jnp.float32),
            jnp.zeros((1, span), jnp.float32),
            jnp.zeros((HD, span), jnp.float32),
        )
        state = lax.fori_loop(0, (live + ROWS - 1) // ROWS, step, state)
        _, total, acc = lax.fori_loop(0, ROWS // (2 * HD), new_step, state)
        write(acc, total, sub)

    bad = jnp.maximum(finish(state_a, parity), finish(state_b, 1 - parity))

    @pl.when(bad > 0)
    def _():
        load_cache(pieces, places, meta, held, sems)

        def drain(i, carry):
            pltpu.make_async_copy(held.at[i], held.at[i], sems.at[i]).wait()
            return carry

        lax.fori_loop(0, (live + ROWS - 1) // ROWS, drain, 0)
        recompute(q_a, query_a, parity)
        recompute(q_b, query_b, 1 - parity)


def attention_call(kernel, meta, arrays, pieces, places, out_shape):
    span = SPAN // 2
    n = NC * CHIPS
    vmem = pl.BlockSpec(memory_space=pltpu.VMEM)
    return pl.pallas_call(
        functools.partial(kernel, places),
        in_specs=[pl.BlockSpec(memory_space=pltpu.SMEM)]
        + [vmem] * len(arrays)
        + [pl.BlockSpec(memory_space=pl.ANY)] * len(pieces),
        out_specs=jax.tree.map(lambda _: vmem, out_shape),
        out_shape=out_shape,
        scratch_shapes=[
            pltpu.VMEM((n, 2 * ROWS, HD), jnp.bfloat16),
            pltpu.SemaphoreType.DMA((n,)),
        ],
        compiler_params=pltpu.CompilerParams(vmem_limit_bytes=60 * 2**20),
        cost_estimate=pl.CostEstimate(
            flops=4 * span * HD * ROWS * (n + 1),
            bytes_accessed=2 * n * 2 * ROWS * HD,
            transcendentals=span * ROWS * (n + 1),
        ),
    )(meta, *arrays, *pieces)


def project_kernel(n_parts, meta, *rest):
    parts = rest[:n_parts]
    w_own, w_got, k_own, v_own, kv_got, o_ref, x_ref, kv_ref = rest[n_parts:]
    depth = w_own.shape[0]
    core = meta[0]
    own = pl.ds(pl.multiple_of(core * depth, depth), depth)
    got = pl.ds(pl.multiple_of((1 - core) * depth, depth), depth)

    def times(own_cols, got_cols):
        out = jnp.dot(x_ref[:, own], own_cols, preferred_element_type=jnp.float32)
        out += jnp.dot(x_ref[:, got], got_cols, preferred_element_type=jnp.float32)
        return out * BOOST

    @pl.when(pl.program_id(0) == 0)
    def _():
        first = 0
        for part in parts:
            x_ref[pl.ds(first, part.shape[0]), :] = part[...]
            first += part.shape[0]
        kv_ref[...] = times(jnp.where(core == 0, k_own[...], v_own[...]), kv_got[...])

    out = times(w_own[...], w_got[...])
    heads, span = o_ref.shape[0], x_ref.shape[0]
    kind = span // NC
    few = kind // CHIPS
    for h in range(heads):
        o_ref[h, :span, :] = out[:, h * HD : (h + 1) * HD]
        chip = pl.program_id(0) * heads + h
        for k in range(NC):
            value = kv_ref[pl.ds(pl.multiple_of(k * kind + chip * few, few), few), :]
            wide = value * 8193.0
            high = wide - (wide - value)
            high = jnp.where(jnp.abs(value) < 2.0**-14, 0.0, high)
            o_ref[h, pl.ds(span + k * few, few), :] = high
            o_ref[h, pl.ds(span + (NC + k) * few, few), :] = (value - high) * LOW


def project(core, parts, q_weight, k_weight, v_weight, got):
    depth, width = q_weight.shape[0], q_weight.shape[1] // NC
    span = sum(part.shape[0] for part in parts)
    tile = 2 * HD
    steps = width // tile
    rows = span + 2 * span // CHIPS
    whole = lambda n, m: (0, 0)
    return pl.pallas_call(
        functools.partial(project_kernel, len(parts)),
        grid_spec=pltpu.PrefetchScalarGridSpec(
            num_scalar_prefetch=1,
            grid=(steps,),
            in_specs=[pl.BlockSpec(part.shape, whole) for part in parts]
            + [
                pl.BlockSpec((depth, tile), lambda n, m: (0, m[0] * steps + n)),
                pl.BlockSpec((depth, tile), lambda n, m: (0, n)),
                pl.BlockSpec((depth, HD), whole),
                pl.BlockSpec((depth, HD), whole),
                pl.BlockSpec((depth, HD), whole),
            ],
            out_specs=pl.BlockSpec((tile // HD, rows, HD), lambda n, m: (n, 0, 0)),
            scratch_shapes=[
                pltpu.VMEM((span, NC * depth), jnp.bfloat16),
                pltpu.VMEM((span, HD), jnp.float32),
            ],
        ),
        out_shape=jax.ShapeDtypeStruct((width // HD, rows, HD), jnp.float32),
        compiler_params=pltpu.CompilerParams(vmem_limit_bytes=24 * 2**20),
        cost_estimate=pl.CostEstimate(
            flops=4 * span * depth * width,
            bytes_accessed=4 * span * depth + 4 * depth * width + 4 * span * width,
            transcendentals=0,
        ),
    )(core[None], *parts, q_weight, got[0], k_weight, v_weight, got[1])


def settle_kernel(meta, sum_a, sum_b, cos_ref, sin_ref, o_ref, rows):
    core, parity = meta[0], meta[1]
    few = cos_ref.shape[0] // 4
    for sub, sums in ((parity, sum_a), (1 - parity, sum_b)):
        start = sums.shape[0] - 2 * NC * few
        for k, kind in enumerate((core, 1 - core)):
            high = sums[start + k * few : start + (k + 1) * few, :]
            low = sums[start + (NC + k) * few : start + (NC + k + 1) * few, :]
            first = pl.multiple_of((2 * kind + sub) * few, few)
            rows[pl.ds(first, few), :] = (high + low * (1.0 / LOW)) * (1.0 / BOOST)
    value = rows[...]
    key = value * cos_ref[...] + pltpu.roll(value, HD // 2, 1) * sin_ref[...]
    out = jnp.where(core == 0, key, jnp.transpose(value)).astype(jnp.bfloat16)
    for i in range(o_ref.shape[0]):
        o_ref[i] = out


def settle(core, parity, sum_a, sum_b, cos_t, sin_t):
    vmem = pl.BlockSpec(memory_space=pltpu.VMEM)
    return pl.pallas_call(
        settle_kernel,
        in_specs=[pl.BlockSpec(memory_space=pltpu.SMEM)] + [vmem] * 4,
        out_specs=vmem,
        out_shape=jax.ShapeDtypeStruct((NC * CHIPS, HD, HD), jnp.bfloat16),
        scratch_shapes=[pltpu.VMEM((HD, HD), jnp.float32)],
    )(jnp.stack([core, parity]), sum_a, sum_b, cos_t, sin_t)


def tables(positions):
    angles = angle_table(positions, HD)
    cos_t, sin_t = jnp.cos(angles), jnp.sin(angles)
    return jnp.concatenate([cos_t, cos_t], axis=1), jnp.concatenate([-sin_t, sin_t], axis=1)


def trade(values, axis):
    return lax.all_to_all(
        values,
        "ulysses",
        split_axis=axis,
        concat_axis=axis,
        axis_index_groups=SAME_CORE,
        tiled=True,
    )


def on_device(
    tokens, q_weight, k_weight, v_weight, cache_keys, cache_values, cache_len, span_start
):
    barrier = lax.optimization_barrier
    n_tensor = lax.axis_size("tensor")
    me = lax.axis_index("ulysses").astype(jnp.int32)
    core = me % NC
    chip = me // NC
    parity = lax.axis_index("tensor").astype(jnp.int32) % 2
    own_rows, features = tokens.shape
    few = own_rows // 2
    depth, width = q_weight.shape[0], q_weight.shape[1] // NC

    cols = jnp.transpose(cache_values.reshape(ROWS // HD, HD, HD), (0, 2, 1)).reshape(ROWS, HD)
    b000 = jnp.concatenate([cache_keys, cols], axis=0)
    b300 = hop(b000, dz=1)
    b100 = hop(b000, dz=-1)
    b010 = hop(b000, dx=1)

    part = lax.dynamic_slice_in_dim(tokens, parity * few, few, 0)
    mine = trade(
        jnp.transpose(part.reshape(few, CHIPS, NC * depth), (1, 0, 2)), 0
    ).reshape(CHIPS * few, NC * depth)

    near = jnp.arange(few, dtype=jnp.int32)[None, None, :]
    kinds = jnp.stack([core, 1 - core])[:, None, None]
    of_chip = jnp.arange(CHIPS, dtype=jnp.int32)[None, :, None]
    index = (of_chip * 4 * few + kinds * 2 * few + near).reshape(-1) + span_start[0]
    turn_a = tables(index + parity * few)
    turn_b = tables(index + (1 - parity) * few)
    turn_kv = tables(
        span_start[0] + chip * 4 * few + jnp.arange(4 * few, dtype=jnp.int32)
    )

    q_got = hop(lax.dynamic_slice_in_dim(q_weight, (1 - core) * width, width, 1), dc=1)
    kv_got = hop(jnp.where(core == 0, v_weight, k_weight), dc=1)
    got = (q_got, kv_got)

    mine, got, b300, b100, b010, turn_a, turn_b, turn_kv = barrier(
        (mine, got, b300, b100, b010, turn_a, turn_b, turn_kv)
    )
    far = CHIPS * few // 2
    other = [hop_y(mine[:far], 1), hop_y(mine[far:], -1)]
    mine_twin = hop(mine, dc=1)

    def sums(parts):
        return project(core, parts, q_weight, k_weight, v_weight, got).astype(jnp.float16)

    half = SPAN // 2

    def total_of(parts):
        return jnp.sum(parts.astype(jnp.float32), axis=0)

    b310 = hop(b010, dz=1)
    b200 = hop(b100, dz=-1)
    b110 = hop(b100, dx=1)
    first_own = [b000, b300, b100, b010]

    sent_a = trade(sums([mine, mine_twin]), 0)
    other, b310, b200, b110 = barrier((other, b310, b200, b110))
    other_twin = [hop(x, dc=1) for x in other]
    first_swap = [hop(b, dc=1) for b in first_own]
    q_b = sums(other + other_twin)
    second_own = [b310, b200, b110]
    second_swap = [hop(b, dc=1) for b in second_own]
    q_b, first_swap, second_swap = barrier((q_b, first_swap, second_swap))
    sent_b = trade(q_b, 0)

    z_me, x_me = chip // NX, chip % NX
    pieces, places, slots = [], [], []

    def add(own, swap, dz, dx, first=0, fresh=True):
        if fresh:
            place = ((z_me + dz) % NZ) * NX * NC + ((x_me + dx) % NX) * NC
            slots.extend([place + core, place + 1 - core])
        pieces.extend([own, swap])
        places.extend([(len(slots) - 2, first, dz), (len(slots) - 1, first, dz)])

    for own, swap, (dz, dx) in zip(
        first_own + second_own,
        first_swap + second_swap,
        [(0, 0), (3, 0), (1, 0), (0, 1), (3, 1), (2, 0), (1, 1)],
    ):
        add(own, swap, dz, dx)
    late = ((z_me + 2) % NZ) * NX + 1 - x_me
    meta = jnp.stack([cache_len[0], core, parity, z_me, late] + slots + [2 * late + core, 2 * late + 1 - core]).astype(jnp.int32)

    shapes = (
        jax.ShapeDtypeStruct((HD, half), jnp.float32),
        jax.ShapeDtypeStruct((8, half), jnp.float32),
        jax.ShapeDtypeStruct((half, HD), jnp.bfloat16),
    )
    sum_a = total_of(sent_a)
    acc_a, total_a, turned_a = attention_call(
        first_kernel, meta, [sum_a, *turn_a], pieces, tuple(places), shapes
    )

    b210k = hop(b200[:ROWS], dx=1)
    b210v = hop(b310[ROWS:], dz=1)
    sent_b, acc_a, total_a, turned_a, b210k, b210v = barrier(
        (sent_b, acc_a, total_a, turned_a, b210k, b210v)
    )
    add(b210k, hop(b210k, dc=1), 2, 1)
    add(b210v, hop(b210v, dc=1), 2, 1, ROWS, False)
    places = tuple(places)
    sum_b = total_of(sent_b)
    *state_b, acc_a, total_a = attention_call(
        second_kernel,
        meta,
        [sum_b, *turn_b, acc_a, total_a, turned_a],
        pieces,
        places,
        shapes + shapes[:2],
    )
    state_a = (acc_a, total_a, turned_a)

    settled = settle(core, parity, sum_a, sum_b, *turn_kv)
    new = lax.all_to_all(settled, "ulysses", split_axis=0, concat_axis=0, tiled=True)
    new, state_b = barrier((new, state_b))
    mixed = attention_call(
        last_kernel,
        meta,
        [*state_a, *state_b, new],
        pieces,
        places,
        jax.ShapeDtypeStruct((CHIPS, NC, 2, few, HD), jnp.bfloat16),
    )
    n_all = n_tensor * NC * CHIPS
    out_rows = SPAN // n_all
    moved = lax.all_to_all(
        mixed.reshape(n_all, out_rows, HD),
        ("tensor", "ulysses"),
        split_axis=0,
        concat_axis=0,
        tiled=True,
    )
    moved = moved.reshape(n_tensor, CHIPS, NC, out_rows, HD)
    return jnp.transpose(moved, (3, 0, 2, 1, 4)).reshape(out_rows, n_all * HD)


def solution(mesh):
    placed = (
        P("ulysses", None),
        P("ulysses", "tensor"),
        P("ulysses", "tensor"),
        P("ulysses", "tensor"),
        P("ulysses", "tensor"),
        P("ulysses", "tensor"),
        P(),
        P(),
    )
    return jax.shard_map(
        on_device,
        mesh=mesh,
        in_specs=placed,
        out_specs=P(("tensor", "ulysses"), None),
        check_vma=False,
    )
```

```python
import functools
import math

import jax
import jax.numpy as jnp
from jax import lax
from jax.experimental import pallas as pl
from jax.experimental.pallas import tpu as pltpu
from jax.sharding import PartitionSpec as P

HD = 128
NZ, NX, NC = 4, 2, 2
CHIPS = NZ * NX
NY = 4
META = 4
SPAN = 1024
ROWS = 1024
SCALE2 = math.log2(math.e) / math.sqrt(HD)
BOOST = 64.0
LOW = 2048.0
NEG = -1e30


def angle_table(positions, head_size):
    steps = jnp.arange(head_size // 2).astype(jnp.float32)
    freq = jnp.exp(-(2.0 * steps / head_size) * math.log(500000.0))
    return positions.astype(jnp.float32)[:, None] * freq[None, :]


def rotate(values, cos_t, sin_t, axis):
    first, second = jnp.split(values, 2, axis=axis)
    return jnp.concatenate(
        [first * cos_t - second * sin_t, second * cos_t + first * sin_t], axis=axis
    )


def unit(z, x, c):
    return (z % NZ) * NX * NC + (x % NX) * NC + c % NC


def hop(values, dz=0, dx=0, dc=0):
    pairs = [
        (unit(z, x, c), unit(z + dz, x + dx, c + dc))
        for z in range(NZ)
        for x in range(NX)
        for c in range(NC)
    ]
    return lax.ppermute(values, "ulysses", pairs)


def hop_y(values, dy):
    pairs = [(x * NY + y, x * NY + (y + dy) % NY) for x in range(2) for y in range(NY)]
    return lax.ppermute(values, "tensor", pairs)


SAME_CORE = [[NC * p + c for p in range(CHIPS)] for c in range(NC)]


def chunk_cols(block, first, count):
    parts = [block[pl.ds(first + HD * i, HD), :] for i in range(count)]
    return jnp.concatenate(parts, axis=1)


def trans_dot(keys, q):
    return lax.dot_general(keys, q, (((1,), (1,)), ((), ())), preferred_element_type=jnp.float32)


def add_values(cols, p):
    return lax.dot_general(
        cols, p.astype(jnp.bfloat16), (((1,), (0,)), ((), ())), preferred_element_type=jnp.float32
    )


def direct(q, keys, cols, state, seen=None):
    acc, total = state
    p = jnp.exp2(trans_dot(keys, q) * SCALE2)
    if seen is not None:
        p = jnp.where(seen(p.shape), p, 0.0)
    folded = jnp.sum(p.reshape(p.shape[0] // 8, 8, p.shape[1]), axis=0)
    return acc + add_values(cols, p), total + folded


def load_cache(pieces, places, meta, held, sems):
    live, z_me = meta[0], meta[3]

    def load(ref, slot, first):
        place = meta[META + slot]

        @pl.when(place * ROWS < live)
        def _():
            rows = pl.ds(first, ref.shape[0])
            pltpu.make_async_copy(ref, held.at[place, rows], sems.at[place]).start()

    for z in range(NZ):

        @pl.when(z_me == z)
        def _(z=z):
            order = sorted(range(len(places)), key=lambda i: (z + places[i][2]) % NZ)
            for i in order:
                load(pieces[i], *places[i][:2])


def turned(q_ref, cos_ref, sin_ref):
    raw = q_ref[: cos_ref.shape[0], :] * (1.0 / BOOST)
    turned_q = raw * cos_ref[...] + pltpu.roll(raw, HD // 2, 1) * sin_ref[...]
    return turned_q.astype(jnp.bfloat16)


def one_block(q, i, live, held, state):
    block = held.at[i]

    def seen(shape):
        return lax.broadcasted_iota(jnp.int32, shape, 0) + i * ROWS < live

    return direct(q, block[:ROWS, :], chunk_cols(block, ROWS, ROWS // HD), state, seen)


def over_cache(q, live, held, sems, state):
    def wait_for(slot):
        pltpu.make_async_copy(held.at[slot], held.at[slot], sems.at[slot]).wait()

    def pair(i, state):
        wait_for(2 * i)
        wait_for(2 * i + 1)
        a, b = held.at[2 * i], held.at[2 * i + 1]
        keys = jnp.concatenate([a[:ROWS, :], b[:ROWS, :]], axis=0)
        cols = jnp.concatenate(
            [chunk_cols(a, ROWS, ROWS // HD), chunk_cols(b, ROWS, ROWS // HD)], axis=1
        )
        return direct(q, keys, cols, state)

    def single(i, state):
        wait_for(i)
        return one_block(q, i, live, held, state)

    pairs = live // (2 * ROWS)
    used = (live + ROWS - 1) // ROWS
    state = lax.fori_loop(0, pairs, pair, state)
    return lax.fori_loop(2 * pairs, used, single, state)


def empty_state(span):
    return jnp.zeros((HD, span), jnp.float32), jnp.zeros((8, span), jnp.float32)


def cache_kernel(places, meta, q_ref, cos_ref, sin_ref, *rest):
    pieces = rest[: len(places)]
    acc_ref, total_ref, turned_ref, held, sems = rest[len(places) :]
    load_cache(pieces, places, meta, held, sems)
    q = turned(q_ref, cos_ref, sin_ref)
    turned_ref[...] = q
    acc, total = over_cache(q, meta[0], held, sems, empty_state(q.shape[0]))
    acc_ref[...] = acc
    total_ref[...] = total


def last_kernel(places, meta, acc_a, total_a, turned_a, acc_b, total_b, turned_b, new_ref, *rest):
    pieces = rest[: len(places)]
    o_ref, held, sems = rest[len(places) :]
    live, core, parity = meta[0], meta[1], meta[2]
    span = turned_a.shape[0]
    part = span // NC
    piece = part // CHIPS

    col = lax.broadcasted_iota(jnp.int32, (1, span), 1)
    kind = jnp.where(col < part, core, 1 - core)
    inside = col % part
    base = (inside // piece) * (4 * piece) + kind * (2 * piece) + inside % piece
    query_a, query_b = base + parity * piece, base + (1 - parity) * piece

    def before(query):
        return lambda shape: lax.broadcasted_iota(jnp.int32, shape, 0) <= query

    new_keys = jnp.concatenate([new_ref[NC * p] for p in range(CHIPS)], axis=0)
    new_cols = jnp.concatenate([new_ref[NC * p + 1] for p in range(CHIPS)], axis=1)
    q_a = turned_a[...]
    state_a = direct(q_a, new_keys, new_cols, (acc_a[...], total_a[...]), before(query_a))
    q_b = turned_b[...]
    state_b = direct(q_b, new_keys, new_cols, (acc_b[...], total_b[...]), before(query_b))

    def write(acc, total, sub):
        out = jnp.transpose(acc / total).astype(jnp.bfloat16)
        for k in range(NC):
            place = core if k == 0 else 1 - core
            for p in range(CHIPS):
                first = k * part + p * piece
                o_ref[p, place, sub] = out[first : first + piece, :]

    def is_bad(total):
        fine = jnp.logical_and(total > 2.0**-60, total < 2.0**110)
        return jnp.max(jnp.where(fine, 0, 1))

    def finish(state, sub):
        acc, total = state
        total = jnp.sum(total, axis=0, keepdims=True)
        write(acc, total, sub)
        return is_bad(total)

    def recompute(q, query, sub):
        def careful(keys, cols, state, seen):
            top, total, acc = state
            s = jnp.where(seen, trans_dot(keys, q), NEG)
            new_top = jnp.maximum(top, jnp.max(s, axis=0, keepdims=True))
            factor = jnp.exp2((top - new_top) * SCALE2)
            p = jnp.where(seen, jnp.exp2((s - new_top) * SCALE2), 0.0)
            total = total * factor + jnp.sum(p, axis=0, keepdims=True)
            return new_top, total, acc * factor + add_values(cols, p)

        def rows_from(first):
            return lax.broadcasted_iota(jnp.int32, (2 * HD, span), 0) + first

        def step(i, state):
            block = held.at[i]

            def inner(j, state):
                first = pl.multiple_of(j * 2 * HD, 2 * HD)
                keys = block[pl.ds(first, 2 * HD), :]
                cols = chunk_cols(block, ROWS + first, 2)
                return careful(keys, cols, state, rows_from(first) + i * ROWS < live)

            return lax.fori_loop(0, ROWS // (2 * HD), inner, state)

        def new_step(j, state):
            first = 2 * NC * j
            keys = jnp.concatenate([new_ref[first], new_ref[first + NC]], axis=0)
            cols = jnp.concatenate([new_ref[first + 1], new_ref[first + NC + 1]], axis=1)
            return careful(keys, cols, state, rows_from(j * 2 * HD) <= query)

        state = (
            jnp.full((1, span), NEG, jnp.float32),
            jnp.zeros((1, span), jnp.float32),
            jnp.zeros((HD, span), jnp.float32),
        )
        state = lax.fori_loop(0, (live + ROWS - 1) // ROWS, step, state)
        _, total, acc = lax.fori_loop(0, ROWS // (2 * HD), new_step, state)
        write(acc, total, sub)

    bad = jnp.maximum(finish(state_a, parity), finish(state_b, 1 - parity))

    @pl.when(bad > 0)
    def _():
        load_cache(pieces, places, meta, held, sems)

        def drain(i, carry):
            pltpu.make_async_copy(held.at[i], held.at[i], sems.at[i]).wait()
            return carry

        lax.fori_loop(0, (live + ROWS - 1) // ROWS, drain, 0)
        recompute(q_a, query_a, parity)
        recompute(q_b, query_b, 1 - parity)


def attention_call(kernel, meta, arrays, pieces, places, out_shape):
    span = SPAN // 2
    n = NC * CHIPS
    vmem = pl.BlockSpec(memory_space=pltpu.VMEM)
    return pl.pallas_call(
        functools.partial(kernel, places),
        in_specs=[pl.BlockSpec(memory_space=pltpu.SMEM)]
        + [vmem] * len(arrays)
        + [pl.BlockSpec(memory_space=pl.ANY)] * len(pieces),
        out_specs=jax.tree.map(lambda _: vmem, out_shape),
        out_shape=out_shape,
        scratch_shapes=[
            pltpu.VMEM((n, 2 * ROWS, HD), jnp.bfloat16),
            pltpu.SemaphoreType.DMA((n,)),
        ],
        compiler_params=pltpu.CompilerParams(vmem_limit_bytes=60 * 2**20),
        cost_estimate=pl.CostEstimate(
            flops=4 * span * HD * ROWS * (n + 1),
            bytes_accessed=2 * n * 2 * ROWS * HD,
            transcendentals=span * ROWS * (n + 1),
        ),
    )(meta, *arrays, *pieces)


def project_kernel(n_parts, meta, *rest):
    parts = rest[:n_parts]
    w_own, w_got, k_own, v_own, kv_got, o_ref, x_ref, kv_ref = rest[n_parts:]
    depth = w_own.shape[0]
    core = meta[0]
    own = pl.ds(pl.multiple_of(core * depth, depth), depth)
    got = pl.ds(pl.multiple_of((1 - core) * depth, depth), depth)

    def times(own_cols, got_cols):
        out = jnp.dot(x_ref[:, own], own_cols, preferred_element_type=jnp.float32)
        out += jnp.dot(x_ref[:, got], got_cols, preferred_element_type=jnp.float32)
        return out * BOOST

    @pl.when(pl.program_id(0) == 0)
    def _():
        first = 0
        for part in parts:
            x_ref[pl.ds(first, part.shape[0]), :] = part[...]
            first += part.shape[0]
        kv_ref[...] = times(jnp.where(core == 0, k_own[...], v_own[...]), kv_got[...])

    out = times(w_own[...], w_got[...])
    heads, span = o_ref.shape[0], x_ref.shape[0]
    kind = span // NC
    few = kind // CHIPS
    for h in range(heads):
        o_ref[h, :span, :] = out[:, h * HD : (h + 1) * HD]
        chip = pl.program_id(0) * heads + h
        for k in range(NC):
            value = kv_ref[pl.ds(pl.multiple_of(k * kind + chip * few, few), few), :]
            wide = value * 8193.0
            high = wide - (wide - value)
            high = jnp.where(jnp.abs(value) < 2.0**-14, 0.0, high)
            o_ref[h, pl.ds(span + k * few, few), :] = high
            o_ref[h, pl.ds(span + (NC + k) * few, few), :] = (value - high) * LOW


def project(core, parts, q_weight, k_weight, v_weight, got):
    depth, width = q_weight.shape[0], q_weight.shape[1] // NC
    span = sum(part.shape[0] for part in parts)
    tile = 2 * HD
    steps = width // tile
    rows = span + 2 * span // CHIPS
    whole = lambda n, m: (0, 0)
    return pl.pallas_call(
        functools.partial(project_kernel, len(parts)),
        grid_spec=pltpu.PrefetchScalarGridSpec(
            num_scalar_prefetch=1,
            grid=(steps,),
            in_specs=[pl.BlockSpec(part.shape, whole) for part in parts]
            + [
                pl.BlockSpec((depth, tile), lambda n, m: (0, m[0] * steps + n)),
                pl.BlockSpec((depth, tile), lambda n, m: (0, n)),
                pl.BlockSpec((depth, HD), whole),
                pl.BlockSpec((depth, HD), whole),
                pl.BlockSpec((depth, HD), whole),
            ],
            out_specs=pl.BlockSpec((tile // HD, rows, HD), lambda n, m: (n, 0, 0)),
            scratch_shapes=[
                pltpu.VMEM((span, NC * depth), jnp.bfloat16),
                pltpu.VMEM((span, HD), jnp.float32),
            ],
        ),
        out_shape=jax.ShapeDtypeStruct((width // HD, rows, HD), jnp.float32),
        compiler_params=pltpu.CompilerParams(vmem_limit_bytes=24 * 2**20),
        cost_estimate=pl.CostEstimate(
            flops=4 * span * depth * width,
            bytes_accessed=4 * span * depth + 4 * depth * width + 4 * span * width,
            transcendentals=0,
        ),
    )(core[None], *parts, q_weight, got[0], k_weight, v_weight, got[1])


def settle_kernel(meta, sum_a, sum_b, cos_ref, sin_ref, o_ref, rows):
    core, parity = meta[0], meta[1]
    few = cos_ref.shape[0] // 4
    for sub, sums in ((parity, sum_a), (1 - parity, sum_b)):
        start = sums.shape[0] - 2 * NC * few
        for k, kind in enumerate((core, 1 - core)):
            high = sums[start + k * few : start + (k + 1) * few, :]
            low = sums[start + (NC + k) * few : start + (NC + k + 1) * few, :]
            first = pl.multiple_of((2 * kind + sub) * few, few)
            rows[pl.ds(first, few), :] = (high + low * (1.0 / LOW)) * (1.0 / BOOST)
    value = rows[...]
    key = value * cos_ref[...] + pltpu.roll(value, HD // 2, 1) * sin_ref[...]
    out = jnp.where(core == 0, key, jnp.transpose(value)).astype(jnp.bfloat16)
    for i in range(o_ref.shape[0]):
        o_ref[i] = out


def settle(core, parity, sum_a, sum_b, cos_t, sin_t):
    vmem = pl.BlockSpec(memory_space=pltpu.VMEM)
    return pl.pallas_call(
        settle_kernel,
        in_specs=[pl.BlockSpec(memory_space=pltpu.SMEM)] + [vmem] * 4,
        out_specs=vmem,
        out_shape=jax.ShapeDtypeStruct((NC * CHIPS, HD, HD), jnp.bfloat16),
        scratch_shapes=[pltpu.VMEM((HD, HD), jnp.float32)],
    )(jnp.stack([core, parity]), sum_a, sum_b, cos_t, sin_t)


def tables(positions):
    angles = angle_table(positions, HD)
    cos_t, sin_t = jnp.cos(angles), jnp.sin(angles)
    return jnp.concatenate([cos_t, cos_t], axis=1), jnp.concatenate([-sin_t, sin_t], axis=1)


def trade(values, axis):
    return lax.all_to_all(
        values,
        "ulysses",
        split_axis=axis,
        concat_axis=axis,
        axis_index_groups=SAME_CORE,
        tiled=True,
    )


def on_device(
    tokens, q_weight, k_weight, v_weight, cache_keys, cache_values, cache_len, span_start
):
    barrier = lax.optimization_barrier
    n_tensor = lax.axis_size("tensor")
    me = lax.axis_index("ulysses").astype(jnp.int32)
    core = me % NC
    chip = me // NC
    parity = lax.axis_index("tensor").astype(jnp.int32) % 2
    own_rows, features = tokens.shape
    few = own_rows // 2
    depth, width = q_weight.shape[0], q_weight.shape[1] // NC

    cols = jnp.transpose(cache_values.reshape(ROWS // HD, HD, HD), (0, 2, 1)).reshape(ROWS, HD)
    b000 = jnp.concatenate([cache_keys, cols], axis=0)
    b300 = hop(b000, dz=1)
    b100 = hop(b000, dz=-1)
    b010 = hop(b000, dx=1)

    part = lax.dynamic_slice_in_dim(tokens, parity * few, few, 0)
    mine = trade(
        jnp.transpose(part.reshape(few, CHIPS, NC * depth), (1, 0, 2)), 0
    ).reshape(CHIPS * few, NC * depth)

    near = jnp.arange(few, dtype=jnp.int32)[None, None, :]
    kinds = jnp.stack([core, 1 - core])[:, None, None]
    of_chip = jnp.arange(CHIPS, dtype=jnp.int32)[None, :, None]
    index = (of_chip * 4 * few + kinds * 2 * few + near).reshape(-1) + span_start[0]
    turn_a = tables(index + parity * few)
    turn_b = tables(index + (1 - parity) * few)
    turn_kv = tables(
        span_start[0] + chip * 4 * few + jnp.arange(4 * few, dtype=jnp.int32)
    )

    q_got = hop(lax.dynamic_slice_in_dim(q_weight, (1 - core) * width, width, 1), dc=1)
    kv_got = hop(jnp.where(core == 0, v_weight, k_weight), dc=1)
    got = (q_got, kv_got)

    mine, got, b300, b100, b010, turn_a, turn_b, turn_kv = barrier(
        (mine, got, b300, b100, b010, turn_a, turn_b, turn_kv)
    )
    far = CHIPS * few // 2
    other = [hop_y(mine[:far], 1), hop_y(mine[far:], -1)]
    mine_twin = hop(mine, dc=1)

    def sums(parts):
        return project(core, parts, q_weight, k_weight, v_weight, got).astype(jnp.float16)

    half = SPAN // 2

    def total_of(parts):
        return jnp.sum(parts.astype(jnp.float32), axis=0)

    b310 = hop(b010, dz=1)
    b200 = hop(b100, dz=-1)
    b110 = hop(b100, dx=1)
    first_own = [b000, b300, b100, b010]

    sent_a = trade(sums([mine, mine_twin]), 0)
    other, b310, b200, b110 = barrier((other, b310, b200, b110))
    other_twin = [hop(x, dc=1) for x in other]
    first_swap = [hop(b, dc=1) for b in first_own]
    q_b = sums(other + other_twin)

    cut = ROWS
    b210 = [hop(b200[:cut], dx=1), hop(b310[cut:], dz=1)]
    sum_a = total_of(sent_a)
    q_b, sum_a, first_swap, b210 = barrier((q_b, sum_a, first_swap, b210))
    sent_b = trade(q_b, 0)
    second_own = [b310, b200, b110]
    second_swap = [hop(b, dc=1) for b in second_own]

    z_me, x_me = chip // NX, chip % NX
    pieces, places, slots = [], [], []

    def add(own, swap, dz, dx, first=0, fresh=True):
        if fresh:
            place = ((z_me + dz) % NZ) * NX * NC + ((x_me + dx) % NX) * NC
            slots.extend([place + core, place + 1 - core])
        pieces.extend([own, swap])
        places.extend([(len(slots) - 2, first, dz), (len(slots) - 1, first, dz)])

    for own, swap, (dz, dx) in zip(
        first_own + second_own,
        first_swap + second_swap,
        [(0, 0), (3, 0), (1, 0), (0, 1), (3, 1), (2, 0), (1, 1)],
    ):
        add(own, swap, dz, dx)
    for i, part in enumerate(b210):
        add(part, hop(part, dc=1), 2, 1, i * cut, i == 0)
    places = tuple(places)
    meta = jnp.stack([cache_len[0], core, parity, z_me] + slots).astype(jnp.int32)

    shapes = (
        jax.ShapeDtypeStruct((HD, half), jnp.float32),
        jax.ShapeDtypeStruct((8, half), jnp.float32),
        jax.ShapeDtypeStruct((half, HD), jnp.bfloat16),
    )
    def attend(sums, turn):
        return attention_call(cache_kernel, meta, [sums, *turn], pieces, places, shapes)

    state_a = attend(sum_a, turn_a)
    sent_b, state_a = barrier((sent_b, state_a))
    sum_b = total_of(sent_b)
    state_b = attend(sum_b, turn_b)

    settled = settle(core, parity, sum_a, sum_b, *turn_kv)
    new = lax.all_to_all(settled, "ulysses", split_axis=0, concat_axis=0, tiled=True)
    new, state_b = barrier((new, state_b))
    mixed = attention_call(
        last_kernel,
        meta,
        [*state_a, *state_b, new],
        pieces,
        places,
        jax.ShapeDtypeStruct((CHIPS, NC, 2, few, HD), jnp.bfloat16),
    )
    n_all = n_tensor * NC * CHIPS
    out_rows = SPAN // n_all
    moved = lax.all_to_all(
        mixed.reshape(n_all, out_rows, HD),
        ("tensor", "ulysses"),
        split_axis=0,
        concat_axis=0,
        tiled=True,
    )
    moved = moved.reshape(n_tensor, CHIPS, NC, out_rows, HD)
    return jnp.transpose(moved, (3, 0, 2, 1, 4)).reshape(out_rows, n_all * HD)


def solution(mesh):
    placed = (
        P("ulysses", None),
        P("ulysses", "tensor"),
        P("ulysses", "tensor"),
        P("ulysses", "tensor"),
        P("ulysses", "tensor"),
        P("ulysses", "tensor"),
        P(),
        P(),
    )
    return jax.shard_map(
        on_device,
        mesh=mesh,
        in_specs=placed,
        out_specs=P(("tensor", "ulysses"), None),
        check_vma=False,
    )
```

```python
import functools
import math

import jax
import jax.numpy as jnp
from jax import lax
from jax.experimental import pallas as pl
from jax.experimental.pallas import tpu as pltpu
from jax.sharding import PartitionSpec as P

HD = 128
NZ, NX, NC = 4, 2, 2
CHIPS = NZ * NX
NY = 4
META = 4
SPAN = 1024
ROWS = 1024
SCALE2 = math.log2(math.e) / math.sqrt(HD)
BOOST = 64.0
LOW = 2048.0
NEG = -1e30


def angle_table(positions, head_size):
    steps = jnp.arange(head_size // 2).astype(jnp.float32)
    freq = jnp.exp(-(2.0 * steps / head_size) * math.log(500000.0))
    return positions.astype(jnp.float32)[:, None] * freq[None, :]


def rotate(values, cos_t, sin_t, axis):
    first, second = jnp.split(values, 2, axis=axis)
    return jnp.concatenate(
        [first * cos_t - second * sin_t, second * cos_t + first * sin_t], axis=axis
    )


def unit(z, x, c):
    return (z % NZ) * NX * NC + (x % NX) * NC + c % NC


def hop(values, dz=0, dx=0, dc=0):
    pairs = [
        (unit(z, x, c), unit(z + dz, x + dx, c + dc))
        for z in range(NZ)
        for x in range(NX)
        for c in range(NC)
    ]
    return lax.ppermute(values, "ulysses", pairs)


def hop_y(values, dy):
    pairs = [(x * NY + y, x * NY + (y + dy) % NY) for x in range(2) for y in range(NY)]
    return lax.ppermute(values, "tensor", pairs)


SAME_CORE = [[NC * p + c for p in range(CHIPS)] for c in range(NC)]


def chunk_cols(block, first, count):
    parts = [block[pl.ds(first + HD * i, HD), :] for i in range(count)]
    return jnp.concatenate(parts, axis=1)


def trans_dot(keys, q):
    return lax.dot_general(keys, q, (((1,), (1,)), ((), ())), preferred_element_type=jnp.float32)


def add_values(cols, p):
    return lax.dot_general(
        cols, p.astype(jnp.bfloat16), (((1,), (0,)), ((), ())), preferred_element_type=jnp.float32
    )


def direct(q, keys, cols, state, seen=None):
    acc, total = state
    p = jnp.exp2(trans_dot(keys, q) * SCALE2)
    if seen is not None:
        p = jnp.where(seen(p.shape), p, 0.0)
    folded = jnp.sum(p.reshape(p.shape[0] // 8, 8, p.shape[1]), axis=0)
    return acc + add_values(cols, p), total + folded


def load_cache(pieces, places, meta, held, sems):
    live, z_me = meta[0], meta[3]

    def load(ref, slot, first):
        place = meta[META + slot]

        @pl.when(place * ROWS < live)
        def _():
            rows = pl.ds(first, ref.shape[0])
            pltpu.make_async_copy(ref, held.at[place, rows], sems.at[place]).start()

    for z in range(NZ):

        @pl.when(z_me == z)
        def _(z=z):
            order = sorted(range(len(places)), key=lambda i: (z + places[i][2]) % NZ)
            for i in order:
                load(pieces[i], *places[i][:2])


def turned(q_ref, cos_ref, sin_ref):
    raw = q_ref[: cos_ref.shape[0], :] * (1.0 / BOOST)
    turned_q = raw * cos_ref[...] + pltpu.roll(raw, HD // 2, 1) * sin_ref[...]
    return turned_q.astype(jnp.bfloat16)


def one_block(q, i, live, held, state):
    block = held.at[i]

    def seen(shape):
        return lax.broadcasted_iota(jnp.int32, shape, 0) + i * ROWS < live

    return direct(q, block[:ROWS, :], chunk_cols(block, ROWS, ROWS // HD), state, seen)


def over_cache(q, live, held, sems, state):
    def wait_for(slot):
        pltpu.make_async_copy(held.at[slot], held.at[slot], sems.at[slot]).wait()

    def several(count):
        def step(i, state):
            for j in range(count):
                wait_for(count * i + j)
            parts = [held.at[count * i + j] for j in range(count)]
            keys = jnp.concatenate([part[:ROWS, :] for part in parts], axis=0)
            cols = [chunk_cols(part, ROWS, ROWS // HD) for part in parts]
            return direct(q, keys, jnp.concatenate(cols, axis=1), state)

        return step

    def single(i, state):
        wait_for(i)
        return one_block(q, i, live, held, state)

    pairs = live // (2 * ROWS)
    used = (live + ROWS - 1) // ROWS
    fours = live // (4 * ROWS)
    state = lax.fori_loop(0, fours, several(4), state)
    state = lax.fori_loop(2 * fours, pairs, several(2), state)
    return lax.fori_loop(2 * pairs, used, single, state)


def empty_state(span):
    return jnp.zeros((HD, span), jnp.float32), jnp.zeros((8, span), jnp.float32)


def cache_kernel(places, meta, q_ref, cos_ref, sin_ref, *rest):
    pieces = rest[: len(places)]
    acc_ref, total_ref, turned_ref, held, sems = rest[len(places) :]
    load_cache(pieces, places, meta, held, sems)
    q = turned(q_ref, cos_ref, sin_ref)
    turned_ref[...] = q
    acc, total = over_cache(q, meta[0], held, sems, empty_state(q.shape[0]))
    acc_ref[...] = acc
    total_ref[...] = total


def last_kernel(places, meta, acc_a, total_a, turned_a, acc_b, total_b, turned_b, new_ref, *rest):
    pieces = rest[: len(places)]
    o_ref, held, sems = rest[len(places) :]
    live, core, parity = meta[0], meta[1], meta[2]
    span = turned_a.shape[0]
    part = span // NC
    piece = part // CHIPS

    col = lax.broadcasted_iota(jnp.int32, (1, span), 1)
    kind = jnp.where(col < part, core, 1 - core)
    inside = col % part
    base = (inside // piece) * (4 * piece) + kind * (2 * piece) + inside % piece
    query_a, query_b = base + parity * piece, base + (1 - parity) * piece

    def before(query):
        return lambda shape: lax.broadcasted_iota(jnp.int32, shape, 0) <= query

    new_keys = jnp.concatenate([new_ref[NC * p] for p in range(CHIPS)], axis=0)
    new_cols = jnp.concatenate([new_ref[NC * p + 1] for p in range(CHIPS)], axis=1)
    q_a = turned_a[...]
    state_a = direct(q_a, new_keys, new_cols, (acc_a[...], total_a[...]), before(query_a))
    q_b = turned_b[...]
    state_b = direct(q_b, new_keys, new_cols, (acc_b[...], total_b[...]), before(query_b))

    def write(acc, total, sub):
        out = jnp.transpose(acc / total).astype(jnp.bfloat16)
        for k in range(NC):
            place = core if k == 0 else 1 - core
            for p in range(CHIPS):
                first = k * part + p * piece
                o_ref[p, place, sub] = out[first : first + piece, :]

    def is_bad(total):
        fine = jnp.logical_and(total > 2.0**-60, total < 2.0**110)
        return jnp.max(jnp.where(fine, 0, 1))

    def finish(state, sub):
        acc, total = state
        total = jnp.sum(total, axis=0, keepdims=True)
        write(acc, total, sub)
        return is_bad(total)

    def recompute(q, query, sub):
        def careful(keys, cols, state, seen):
            top, total, acc = state
            s = jnp.where(seen, trans_dot(keys, q), NEG)
            new_top = jnp.maximum(top, jnp.max(s, axis=0, keepdims=True))
            factor = jnp.exp2((top - new_top) * SCALE2)
            p = jnp.where(seen, jnp.exp2((s - new_top) * SCALE2), 0.0)
            total = total * factor + jnp.sum(p, axis=0, keepdims=True)
            return new_top, total, acc * factor + add_values(cols, p)

        def rows_from(first):
            return lax.broadcasted_iota(jnp.int32, (2 * HD, span), 0) + first

        def step(i, state):
            block = held.at[i]

            def inner(j, state):
                first = pl.multiple_of(j * 2 * HD, 2 * HD)
                keys = block[pl.ds(first, 2 * HD), :]
                cols = chunk_cols(block, ROWS + first, 2)
                return careful(keys, cols, state, rows_from(first) + i * ROWS < live)

            return lax.fori_loop(0, ROWS // (2 * HD), inner, state)

        def new_step(j, state):
            first = 2 * NC * j
            keys = jnp.concatenate([new_ref[first], new_ref[first + NC]], axis=0)
            cols = jnp.concatenate([new_ref[first + 1], new_ref[first + NC + 1]], axis=1)
            return careful(keys, cols, state, rows_from(j * 2 * HD) <= query)

        state = (
            jnp.full((1, span), NEG, jnp.float32),
            jnp.zeros((1, span), jnp.float32),
            jnp.zeros((HD, span), jnp.float32),
        )
        state = lax.fori_loop(0, (live + ROWS - 1) // ROWS, step, state)
        _, total, acc = lax.fori_loop(0, ROWS // (2 * HD), new_step, state)
        write(acc, total, sub)

    bad = jnp.maximum(finish(state_a, parity), finish(state_b, 1 - parity))

    @pl.when(bad > 0)
    def _():
        load_cache(pieces, places, meta, held, sems)

        def drain(i, carry):
            pltpu.make_async_copy(held.at[i], held.at[i], sems.at[i]).wait()
            return carry

        lax.fori_loop(0, (live + ROWS - 1) // ROWS, drain, 0)
        recompute(q_a, query_a, parity)
        recompute(q_b, query_b, 1 - parity)


def attention_call(kernel, meta, arrays, pieces, places, out_shape):
    span = SPAN // 2
    n = NC * CHIPS
    vmem = pl.BlockSpec(memory_space=pltpu.VMEM)
    return pl.pallas_call(
        functools.partial(kernel, places),
        in_specs=[pl.BlockSpec(memory_space=pltpu.SMEM)]
        + [vmem] * len(arrays)
        + [pl.BlockSpec(memory_space=pl.ANY)] * len(pieces),
        out_specs=jax.tree.map(lambda _: vmem, out_shape),
        out_shape=out_shape,
        scratch_shapes=[
            pltpu.VMEM((n, 2 * ROWS, HD), jnp.bfloat16),
            pltpu.SemaphoreType.DMA((n,)),
        ],
        compiler_params=pltpu.CompilerParams(vmem_limit_bytes=60 * 2**20),
        cost_estimate=pl.CostEstimate(
            flops=4 * span * HD * ROWS * (n + 1),
            bytes_accessed=2 * n * 2 * ROWS * HD,
            transcendentals=span * ROWS * (n + 1),
        ),
    )(meta, *arrays, *pieces)


def project_kernel(n_parts, meta, *rest):
    parts = rest[:n_parts]
    w_own, w_got, k_own, v_own, kv_got, o_ref, x_ref, kv_ref = rest[n_parts:]
    depth = w_own.shape[0]
    core = meta[0]
    own = pl.ds(pl.multiple_of(core * depth, depth), depth)
    got = pl.ds(pl.multiple_of((1 - core) * depth, depth), depth)

    def times(own_cols, got_cols):
        out = jnp.dot(x_ref[:, own], own_cols, preferred_element_type=jnp.float32)
        out += jnp.dot(x_ref[:, got], got_cols, preferred_element_type=jnp.float32)
        return out * BOOST

    @pl.when(pl.program_id(0) == 0)
    def _():
        first = 0
        for part in parts:
            x_ref[pl.ds(first, part.shape[0]), :] = part[...]
            first += part.shape[0]
        kv_ref[...] = times(jnp.where(core == 0, k_own[...], v_own[...]), kv_got[...])

    out = times(w_own[...], w_got[...])
    heads, span = o_ref.shape[0], x_ref.shape[0]
    kind = span // NC
    few = kind // CHIPS
    for h in range(heads):
        o_ref[h, :span, :] = out[:, h * HD : (h + 1) * HD]
        chip = pl.program_id(0) * heads + h
        for k in range(NC):
            value = kv_ref[pl.ds(pl.multiple_of(k * kind + chip * few, few), few), :]
            wide = value * 8193.0
            high = wide - (wide - value)
            high = jnp.where(jnp.abs(value) < 2.0**-14, 0.0, high)
            o_ref[h, pl.ds(span + k * few, few), :] = high
            o_ref[h, pl.ds(span + (NC + k) * few, few), :] = (value - high) * LOW


def project(core, parts, q_weight, k_weight, v_weight, got):
    depth, width = q_weight.shape[0], q_weight.shape[1] // NC
    span = sum(part.shape[0] for part in parts)
    tile = 2 * HD
    steps = width // tile
    rows = span + 2 * span // CHIPS
    whole = lambda n, m: (0, 0)
    return pl.pallas_call(
        functools.partial(project_kernel, len(parts)),
        grid_spec=pltpu.PrefetchScalarGridSpec(
            num_scalar_prefetch=1,
            grid=(steps,),
            in_specs=[pl.BlockSpec(part.shape, whole) for part in parts]
            + [
                pl.BlockSpec((depth, tile), lambda n, m: (0, m[0] * steps + n)),
                pl.BlockSpec((depth, tile), lambda n, m: (0, n)),
                pl.BlockSpec((depth, HD), whole),
                pl.BlockSpec((depth, HD), whole),
                pl.BlockSpec((depth, HD), whole),
            ],
            out_specs=pl.BlockSpec((tile // HD, rows, HD), lambda n, m: (n, 0, 0)),
            scratch_shapes=[
                pltpu.VMEM((span, NC * depth), jnp.bfloat16),
                pltpu.VMEM((span, HD), jnp.float32),
            ],
        ),
        out_shape=jax.ShapeDtypeStruct((width // HD, rows, HD), jnp.float32),
        compiler_params=pltpu.CompilerParams(vmem_limit_bytes=24 * 2**20),
        cost_estimate=pl.CostEstimate(
            flops=4 * span * depth * width,
            bytes_accessed=4 * span * depth + 4 * depth * width + 4 * span * width,
            transcendentals=0,
        ),
    )(core[None], *parts, q_weight, got[0], k_weight, v_weight, got[1])


def settle_kernel(meta, sum_a, sum_b, cos_ref, sin_ref, o_ref, rows):
    core, parity = meta[0], meta[1]
    few = cos_ref.shape[0] // 4
    for sub, sums in ((parity, sum_a), (1 - parity, sum_b)):
        start = sums.shape[0] - 2 * NC * few
        for k, kind in enumerate((core, 1 - core)):
            high = sums[start + k * few : start + (k + 1) * few, :]
            low = sums[start + (NC + k) * few : start + (NC + k + 1) * few, :]
            first = pl.multiple_of((2 * kind + sub) * few, few)
            rows[pl.ds(first, few), :] = (high + low * (1.0 / LOW)) * (1.0 / BOOST)
    value = rows[...]
    key = value * cos_ref[...] + pltpu.roll(value, HD // 2, 1) * sin_ref[...]
    out = jnp.where(core == 0, key, jnp.transpose(value)).astype(jnp.bfloat16)
    for i in range(o_ref.shape[0]):
        o_ref[i] = out


def settle(core, parity, sum_a, sum_b, cos_t, sin_t):
    vmem = pl.BlockSpec(memory_space=pltpu.VMEM)
    return pl.pallas_call(
        settle_kernel,
        in_specs=[pl.BlockSpec(memory_space=pltpu.SMEM)] + [vmem] * 4,
        out_specs=vmem,
        out_shape=jax.ShapeDtypeStruct((NC * CHIPS, HD, HD), jnp.bfloat16),
        scratch_shapes=[pltpu.VMEM((HD, HD), jnp.float32)],
    )(jnp.stack([core, parity]), sum_a, sum_b, cos_t, sin_t)


def tables(positions):
    angles = angle_table(positions, HD)
    cos_t, sin_t = jnp.cos(angles), jnp.sin(angles)
    return jnp.concatenate([cos_t, cos_t], axis=1), jnp.concatenate([-sin_t, sin_t], axis=1)


def trade(values, axis):
    return lax.all_to_all(
        values,
        "ulysses",
        split_axis=axis,
        concat_axis=axis,
        axis_index_groups=SAME_CORE,
        tiled=True,
    )


def on_device(
    tokens, q_weight, k_weight, v_weight, cache_keys, cache_values, cache_len, span_start
):
    barrier = lax.optimization_barrier
    n_tensor = lax.axis_size("tensor")
    me = lax.axis_index("ulysses").astype(jnp.int32)
    core = me % NC
    chip = me // NC
    parity = lax.axis_index("tensor").astype(jnp.int32) % 2
    own_rows, features = tokens.shape
    few = own_rows // 2
    depth, width = q_weight.shape[0], q_weight.shape[1] // NC

    cols = jnp.transpose(cache_values.reshape(ROWS // HD, HD, HD), (0, 2, 1)).reshape(ROWS, HD)
    b000 = jnp.concatenate([cache_keys, cols], axis=0)
    b300 = hop(b000, dz=1)
    b100 = hop(b000, dz=-1)
    b010 = hop(b000, dx=1)

    part = lax.dynamic_slice_in_dim(tokens, parity * few, few, 0)
    mine = trade(
        jnp.transpose(part.reshape(few, CHIPS, NC * depth), (1, 0, 2)), 0
    ).reshape(CHIPS * few, NC * depth)

    near = jnp.arange(few, dtype=jnp.int32)[None, None, :]
    kinds = jnp.stack([core, 1 - core])[:, None, None]
    of_chip = jnp.arange(CHIPS, dtype=jnp.int32)[None, :, None]
    index = (of_chip * 4 * few + kinds * 2 * few + near).reshape(-1) + span_start[0]
    turn_a = tables(index + parity * few)
    turn_b = tables(index + (1 - parity) * few)
    turn_kv = tables(
        span_start[0] + chip * 4 * few + jnp.arange(4 * few, dtype=jnp.int32)
    )

    q_got = hop(lax.dynamic_slice_in_dim(q_weight, (1 - core) * width, width, 1), dc=1)
    kv_got = hop(jnp.where(core == 0, v_weight, k_weight), dc=1)
    got = (q_got, kv_got)

    mine, got, b300, b100, b010, turn_a, turn_b, turn_kv = barrier(
        (mine, got, b300, b100, b010, turn_a, turn_b, turn_kv)
    )
    far = CHIPS * few // 2
    other = [hop_y(mine[:far], 1), hop_y(mine[far:], -1)]
    mine_twin = hop(mine, dc=1)

    def sums(parts):
        return project(core, parts, q_weight, k_weight, v_weight, got).astype(jnp.float16)

    half = SPAN // 2

    def total_of(parts):
        return jnp.sum(parts.astype(jnp.float32), axis=0)

    b310 = hop(b010, dz=1)
    b200 = hop(b100, dz=-1)
    b110 = hop(b100, dx=1)
    first_own = [b000, b300, b100, b010]

    sent_a = trade(sums([mine, mine_twin]), 0)
    other, b310, b200, b110 = barrier((other, b310, b200, b110))
    other_twin = [hop(x, dc=1) for x in other]
    first_swap = [hop(b, dc=1) for b in first_own]
    q_b = sums(other + other_twin)

    cut = ROWS
    b210 = [hop(b200[:cut], dx=1), hop(b310[cut:], dz=1)]
    sum_a = total_of(sent_a)
    q_b, sum_a, first_swap, b210 = barrier((q_b, sum_a, first_swap, b210))
    sent_b = trade(q_b, 0)
    second_own = [b310, b200, b110]
    second_swap = [hop(b, dc=1) for b in second_own]

    z_me, x_me = chip // NX, chip % NX
    pieces, places, slots = [], [], []

    def add(own, swap, dz, dx, first=0, fresh=True):
        if fresh:
            place = ((z_me + dz) % NZ) * NX * NC + ((x_me + dx) % NX) * NC
            slots.extend([place + core, place + 1 - core])
        pieces.extend([own, swap])
        places.extend([(len(slots) - 2, first, dz), (len(slots) - 1, first, dz)])

    for own, swap, (dz, dx) in zip(
        first_own + second_own,
        first_swap + second_swap,
        [(0, 0), (3, 0), (1, 0), (0, 1), (3, 1), (2, 0), (1, 1)],
    ):
        add(own, swap, dz, dx)
    for i, part in enumerate(b210):
        add(part, hop(part, dc=1), 2, 1, i * cut, i == 0)
    places = tuple(places)
    meta = jnp.stack([cache_len[0], core, parity, z_me] + slots).astype(jnp.int32)

    shapes = (
        jax.ShapeDtypeStruct((HD, half), jnp.float32),
        jax.ShapeDtypeStruct((8, half), jnp.float32),
        jax.ShapeDtypeStruct((half, HD), jnp.bfloat16),
    )
    def attend(sums, turn):
        return attention_call(cache_kernel, meta, [sums, *turn], pieces, places, shapes)

    state_a = attend(sum_a, turn_a)
    sent_b, state_a = barrier((sent_b, state_a))
    sum_b = total_of(sent_b)
    state_b = attend(sum_b, turn_b)

    settled = settle(core, parity, sum_a, sum_b, *turn_kv)
    new = lax.all_to_all(settled, "ulysses", split_axis=0, concat_axis=0, tiled=True)
    new, state_b = barrier((new, state_b))
    mixed = attention_call(
        last_kernel,
        meta,
        [*state_a, *state_b, new],
        pieces,
        places,
        jax.ShapeDtypeStruct((CHIPS, NC, 2, few, HD), jnp.bfloat16),
    )
    n_all = n_tensor * NC * CHIPS
    out_rows = SPAN // n_all
    moved = lax.all_to_all(
        mixed.reshape(n_all, out_rows, HD),
        ("tensor", "ulysses"),
        split_axis=0,
        concat_axis=0,
        tiled=True,
    )
    moved = moved.reshape(n_tensor, CHIPS, NC, out_rows, HD)
    return jnp.transpose(moved, (3, 0, 2, 1, 4)).reshape(out_rows, n_all * HD)


def solution(mesh):
    placed = (
        P("ulysses", None),
        P("ulysses", "tensor"),
        P("ulysses", "tensor"),
        P("ulysses", "tensor"),
        P("ulysses", "tensor"),
        P("ulysses", "tensor"),
        P(),
        P(),
    )
    return jax.shard_map(
        on_device,
        mesh=mesh,
        in_specs=placed,
        out_specs=P(("tensor", "ulysses"), None),
        check_vma=False,
    )
```

```python
import functools
import math

import jax
import jax.numpy as jnp
from jax import lax
from jax.experimental import pallas as pl
from jax.experimental.pallas import tpu as pltpu
from jax.sharding import PartitionSpec as P

HD = 128
NZ, NX, NC = 4, 2, 2
CHIPS = NZ * NX
NY = 4
META = 4
SPAN = 1024
ROWS = 1024
SCALE2 = math.log2(math.e) / math.sqrt(HD)
BOOST = 64.0
LOW = 2048.0
NEG = -1e30


def angle_table(positions, head_size):
    steps = jnp.arange(head_size // 2).astype(jnp.float32)
    freq = jnp.exp(-(2.0 * steps / head_size) * math.log(500000.0))
    return positions.astype(jnp.float32)[:, None] * freq[None, :]


def rotate(values, cos_t, sin_t, axis):
    first, second = jnp.split(values, 2, axis=axis)
    return jnp.concatenate(
        [first * cos_t - second * sin_t, second * cos_t + first * sin_t], axis=axis
    )


def unit(z, x, c):
    return (z % NZ) * NX * NC + (x % NX) * NC + c % NC


def hop(values, dz=0, dx=0, dc=0):
    pairs = [
        (unit(z, x, c), unit(z + dz, x + dx, c + dc))
        for z in range(NZ)
        for x in range(NX)
        for c in range(NC)
    ]
    return lax.ppermute(values, "ulysses", pairs)


def hop_y(values, dy):
    pairs = [(x * NY + y, x * NY + (y + dy) % NY) for x in range(2) for y in range(NY)]
    return lax.ppermute(values, "tensor", pairs)


SAME_CORE = [[NC * p + c for p in range(CHIPS)] for c in range(NC)]


def chunk_cols(block, first, count):
    parts = [block[pl.ds(first + HD * i, HD), :] for i in range(count)]
    return jnp.concatenate(parts, axis=1)


def trans_dot(keys, q):
    return lax.dot_general(keys, q, (((1,), (1,)), ((), ())), preferred_element_type=jnp.float32)


def add_values(cols, p):
    return lax.dot_general(
        cols, p.astype(jnp.bfloat16), (((1,), (0,)), ((), ())), preferred_element_type=jnp.float32
    )


def direct(q, keys, cols, state, seen=None):
    acc, total = state
    p = jnp.exp2(trans_dot(keys, q) * SCALE2)
    if seen is not None:
        p = jnp.where(seen(p.shape), p, 0.0)
    folded = jnp.sum(p.reshape(p.shape[0] // 8, 8, p.shape[1]), axis=0)
    return acc + add_values(cols, p), total + folded


def load_cache(pieces, places, meta, held, sems):
    live, z_me = meta[0], meta[3]

    def load(ref, slot, first):
        place = meta[META + slot]

        @pl.when(place * ROWS < live)
        def _():
            rows = pl.ds(first, ref.shape[0])
            pltpu.make_async_copy(ref, held.at[place, rows], sems.at[place]).start()

    for z in range(NZ):

        @pl.when(z_me == z)
        def _(z=z):
            order = sorted(range(len(places)), key=lambda i: (z + places[i][2]) % NZ)
            for i in order:
                load(pieces[i], *places[i][:2])


def turned(q_ref, cos_ref, sin_ref):
    raw = q_ref[: cos_ref.shape[0], :] * (1.0 / BOOST)
    turned_q = raw * cos_ref[...] + pltpu.roll(raw, HD // 2, 1) * sin_ref[...]
    return turned_q.astype(jnp.bfloat16)


def one_block(q, i, live, held, state):
    block = held.at[i]

    def seen(shape):
        return lax.broadcasted_iota(jnp.int32, shape, 0) + i * ROWS < live

    return direct(q, block[:ROWS, :], chunk_cols(block, ROWS, ROWS // HD), state, seen)


def over_cache(q, live, held, sems, state):
    def wait_for(slot):
        pltpu.make_async_copy(held.at[slot], held.at[slot], sems.at[slot]).wait()

    def pair(i, state):
        wait_for(2 * i)
        wait_for(2 * i + 1)
        a, b = held.at[2 * i], held.at[2 * i + 1]
        keys = jnp.concatenate([a[:ROWS, :], b[:ROWS, :]], axis=0)
        cols = jnp.concatenate(
            [chunk_cols(a, ROWS, ROWS // HD), chunk_cols(b, ROWS, ROWS // HD)], axis=1
        )
        return direct(q, keys, cols, state)

    def single(i, state):
        wait_for(i)
        return one_block(q, i, live, held, state)

    pairs = live // (2 * ROWS)
    used = (live + ROWS - 1) // ROWS
    state = lax.fori_loop(0, pairs, pair, state)
    return lax.fori_loop(2 * pairs, used, single, state)


def empty_state(span):
    return jnp.zeros((HD, span), jnp.float32), jnp.zeros((8, span), jnp.float32)


def cache_kernel(places, meta, q_ref, cos_ref, sin_ref, *rest):
    pieces = rest[: len(places)]
    acc_ref, total_ref, turned_ref, held, sems = rest[len(places) :]
    load_cache(pieces, places, meta, held, sems)
    q = turned(q_ref, cos_ref, sin_ref)
    turned_ref[...] = q
    acc, total = over_cache(q, meta[0], held, sems, empty_state(q.shape[0]))
    acc_ref[...] = acc
    total_ref[...] = total


def last_kernel(places, meta, acc_a, total_a, turned_a, acc_b, total_b, turned_b, own, twin, *rest):
    pieces = rest[: len(places)]
    o_ref, held, sems = rest[len(places) :]
    live, core, parity = meta[0], meta[1], meta[2]
    span = turned_a.shape[0]
    part = span // NC
    piece = part // CHIPS

    col = lax.broadcasted_iota(jnp.int32, (1, span), 1)
    kind = jnp.where(col < part, core, 1 - core)
    inside = col % part
    base = (inside // piece) * (4 * piece) + kind * (2 * piece) + inside % piece
    query_a, query_b = base + parity * piece, base + (1 - parity) * piece

    def before(query):
        return lambda shape: lax.broadcasted_iota(jnp.int32, shape, 0) <= query

    first_is_own = core == 0
    new_keys = jnp.concatenate(
        [jnp.where(first_is_own, own[p], twin[p]) for p in range(CHIPS)], axis=0
    )
    new_cols = jnp.concatenate(
        [jnp.where(first_is_own, twin[p], own[p]) for p in range(CHIPS)], axis=1
    )
    q_a = turned_a[...]
    state_a = direct(q_a, new_keys, new_cols, (acc_a[...], total_a[...]), before(query_a))
    q_b = turned_b[...]
    state_b = direct(q_b, new_keys, new_cols, (acc_b[...], total_b[...]), before(query_b))

    def write(acc, total, sub):
        out = jnp.transpose(acc / total).astype(jnp.bfloat16)
        for k in range(NC):
            place = core if k == 0 else 1 - core
            for p in range(CHIPS):
                first = k * part + p * piece
                o_ref[p, place, sub] = out[first : first + piece, :]

    def is_bad(total):
        fine = jnp.logical_and(total > 2.0**-60, total < 2.0**110)
        return jnp.max(jnp.where(fine, 0, 1))

    def finish(state, sub):
        acc, total = state
        total = jnp.sum(total, axis=0, keepdims=True)
        write(acc, total, sub)
        return is_bad(total)

    def recompute(q, query, sub):
        def careful(keys, cols, state, seen):
            top, total, acc = state
            s = jnp.where(seen, trans_dot(keys, q), NEG)
            new_top = jnp.maximum(top, jnp.max(s, axis=0, keepdims=True))
            factor = jnp.exp2((top - new_top) * SCALE2)
            p = jnp.where(seen, jnp.exp2((s - new_top) * SCALE2), 0.0)
            total = total * factor + jnp.sum(p, axis=0, keepdims=True)
            return new_top, total, acc * factor + add_values(cols, p)

        def rows_from(first):
            return lax.broadcasted_iota(jnp.int32, (2 * HD, span), 0) + first

        def step(i, state):
            block = held.at[i]

            def inner(j, state):
                first = pl.multiple_of(j * 2 * HD, 2 * HD)
                keys = block[pl.ds(first, 2 * HD), :]
                cols = chunk_cols(block, ROWS + first, 2)
                return careful(keys, cols, state, rows_from(first) + i * ROWS < live)

            return lax.fori_loop(0, ROWS // (2 * HD), inner, state)

        def new_step(j, state):
            own_two, twin_two = own[pl.ds(2 * j, 2)], twin[pl.ds(2 * j, 2)]
            keys = jnp.where(first_is_own, own_two, twin_two).reshape(2 * HD, HD)
            cols = jnp.where(first_is_own, twin_two, own_two)
            cols = jnp.concatenate([cols[0], cols[1]], axis=1)
            return careful(keys, cols, state, rows_from(j * 2 * HD) <= query)

        state = (
            jnp.full((1, span), NEG, jnp.float32),
            jnp.zeros((1, span), jnp.float32),
            jnp.zeros((HD, span), jnp.float32),
        )
        state = lax.fori_loop(0, (live + ROWS - 1) // ROWS, step, state)
        _, total, acc = lax.fori_loop(0, ROWS // (2 * HD), new_step, state)
        write(acc, total, sub)

    bad = jnp.maximum(finish(state_a, parity), finish(state_b, 1 - parity))

    @pl.when(bad > 0)
    def _():
        load_cache(pieces, places, meta, held, sems)

        def drain(i, carry):
            pltpu.make_async_copy(held.at[i], held.at[i], sems.at[i]).wait()
            return carry

        lax.fori_loop(0, (live + ROWS - 1) // ROWS, drain, 0)
        recompute(q_a, query_a, parity)
        recompute(q_b, query_b, 1 - parity)


def attention_call(kernel, meta, arrays, pieces, places, out_shape):
    span = SPAN // 2
    n = NC * CHIPS
    vmem = pl.BlockSpec(memory_space=pltpu.VMEM)
    return pl.pallas_call(
        functools.partial(kernel, places),
        in_specs=[pl.BlockSpec(memory_space=pltpu.SMEM)]
        + [vmem] * len(arrays)
        + [pl.BlockSpec(memory_space=pl.ANY)] * len(pieces),
        out_specs=jax.tree.map(lambda _: vmem, out_shape),
        out_shape=out_shape,
        scratch_shapes=[
            pltpu.VMEM((n, 2 * ROWS, HD), jnp.bfloat16),
            pltpu.SemaphoreType.DMA((n,)),
        ],
        compiler_params=pltpu.CompilerParams(vmem_limit_bytes=60 * 2**20),
        cost_estimate=pl.CostEstimate(
            flops=4 * span * HD * ROWS * (n + 1),
            bytes_accessed=2 * n * 2 * ROWS * HD,
            transcendentals=span * ROWS * (n + 1),
        ),
    )(meta, *arrays, *pieces)


def project_kernel(n_parts, meta, *rest):
    parts = rest[:n_parts]
    w_own, w_got, k_own, v_own, kv_got, o_ref, x_ref, kv_ref = rest[n_parts:]
    depth = w_own.shape[0]
    core = meta[0]
    own = pl.ds(pl.multiple_of(core * depth, depth), depth)
    got = pl.ds(pl.multiple_of((1 - core) * depth, depth), depth)

    def times(own_cols, got_cols):
        out = jnp.dot(x_ref[:, own], own_cols, preferred_element_type=jnp.float32)
        out += jnp.dot(x_ref[:, got], got_cols, preferred_element_type=jnp.float32)
        return out * BOOST

    @pl.when(pl.program_id(0) == 0)
    def _():
        first = 0
        for part in parts:
            x_ref[pl.ds(first, part.shape[0]), :] = part[...]
            first += part.shape[0]
        kv_ref[...] = times(jnp.where(core == 0, k_own[...], v_own[...]), kv_got[...])

    out = times(w_own[...], w_got[...])
    heads, span = o_ref.shape[0], x_ref.shape[0]
    kind = span // NC
    few = kind // CHIPS
    for h in range(heads):
        o_ref[h, :span, :] = out[:, h * HD : (h + 1) * HD]
        chip = pl.program_id(0) * heads + h
        for k in range(NC):
            value = kv_ref[pl.ds(pl.multiple_of(k * kind + chip * few, few), few), :]
            wide = value * 8193.0
            high = wide - (wide - value)
            high = jnp.where(jnp.abs(value) < 2.0**-14, 0.0, high)
            o_ref[h, pl.ds(span + k * few, few), :] = high
            o_ref[h, pl.ds(span + (NC + k) * few, few), :] = (value - high) * LOW


def project(core, parts, q_weight, k_weight, v_weight, got):
    depth, width = q_weight.shape[0], q_weight.shape[1] // NC
    span = sum(part.shape[0] for part in parts)
    tile = 2 * HD
    steps = width // tile
    rows = span + 2 * span // CHIPS
    whole = lambda n, m: (0, 0)
    return pl.pallas_call(
        functools.partial(project_kernel, len(parts)),
        grid_spec=pltpu.PrefetchScalarGridSpec(
            num_scalar_prefetch=1,
            grid=(steps,),
            in_specs=[pl.BlockSpec(part.shape, whole) for part in parts]
            + [
                pl.BlockSpec((depth, tile), lambda n, m: (0, m[0] * steps + n)),
                pl.BlockSpec((depth, tile), lambda n, m: (0, n)),
                pl.BlockSpec((depth, HD), whole),
                pl.BlockSpec((depth, HD), whole),
                pl.BlockSpec((depth, HD), whole),
            ],
            out_specs=pl.BlockSpec((tile // HD, rows, HD), lambda n, m: (n, 0, 0)),
            scratch_shapes=[
                pltpu.VMEM((span, NC * depth), jnp.bfloat16),
                pltpu.VMEM((span, HD), jnp.float32),
            ],
        ),
        out_shape=jax.ShapeDtypeStruct((width // HD, rows, HD), jnp.float32),
        compiler_params=pltpu.CompilerParams(vmem_limit_bytes=24 * 2**20),
        cost_estimate=pl.CostEstimate(
            flops=4 * span * depth * width,
            bytes_accessed=4 * span * depth + 4 * depth * width + 4 * span * width,
            transcendentals=0,
        ),
    )(core[None], *parts, q_weight, got[0], k_weight, v_weight, got[1])


def settle_kernel(meta, sum_a, sum_b, cos_ref, sin_ref, o_ref, rows):
    core, parity = meta[0], meta[1]
    few = cos_ref.shape[0] // 4
    for sub, sums in ((parity, sum_a), (1 - parity, sum_b)):
        start = sums.shape[0] - 2 * NC * few
        for k, kind in enumerate((core, 1 - core)):
            high = sums[start + k * few : start + (k + 1) * few, :]
            low = sums[start + (NC + k) * few : start + (NC + k + 1) * few, :]
            first = pl.multiple_of((2 * kind + sub) * few, few)
            rows[pl.ds(first, few), :] = (high + low * (1.0 / LOW)) * (1.0 / BOOST)
    value = rows[...]
    key = value * cos_ref[...] + pltpu.roll(value, HD // 2, 1) * sin_ref[...]
    out = jnp.where(core == 0, key, jnp.transpose(value)).astype(jnp.bfloat16)
    for i in range(o_ref.shape[0]):
        o_ref[i] = out


def settle(core, parity, sum_a, sum_b, cos_t, sin_t):
    vmem = pl.BlockSpec(memory_space=pltpu.VMEM)
    return pl.pallas_call(
        settle_kernel,
        in_specs=[pl.BlockSpec(memory_space=pltpu.SMEM)] + [vmem] * 4,
        out_specs=vmem,
        out_shape=jax.ShapeDtypeStruct((CHIPS, HD, HD), jnp.bfloat16),
        scratch_shapes=[pltpu.VMEM((HD, HD), jnp.float32)],
    )(jnp.stack([core, parity]), sum_a, sum_b, cos_t, sin_t)


def tables(positions):
    angles = angle_table(positions, HD)
    cos_t, sin_t = jnp.cos(angles), jnp.sin(angles)
    return jnp.concatenate([cos_t, cos_t], axis=1), jnp.concatenate([-sin_t, sin_t], axis=1)


def trade(values, axis):
    return lax.all_to_all(
        values,
        "ulysses",
        split_axis=axis,
        concat_axis=axis,
        axis_index_groups=SAME_CORE,
        tiled=True,
    )


def on_device(
    tokens, q_weight, k_weight, v_weight, cache_keys, cache_values, cache_len, span_start
):
    barrier = lax.optimization_barrier
    n_tensor = lax.axis_size("tensor")
    me = lax.axis_index("ulysses").astype(jnp.int32)
    core = me % NC
    chip = me // NC
    parity = lax.axis_index("tensor").astype(jnp.int32) % 2
    own_rows, features = tokens.shape
    few = own_rows // 2
    depth, width = q_weight.shape[0], q_weight.shape[1] // NC

    cols = jnp.transpose(cache_values.reshape(ROWS // HD, HD, HD), (0, 2, 1)).reshape(ROWS, HD)
    b000 = jnp.concatenate([cache_keys, cols], axis=0)
    b300 = hop(b000, dz=1)
    b100 = hop(b000, dz=-1)
    b010 = hop(b000, dx=1)

    part = lax.dynamic_slice_in_dim(tokens, parity * few, few, 0)
    mine = trade(
        jnp.transpose(part.reshape(few, CHIPS, NC * depth), (1, 0, 2)), 0
    ).reshape(CHIPS * few, NC * depth)

    near = jnp.arange(few, dtype=jnp.int32)[None, None, :]
    kinds = jnp.stack([core, 1 - core])[:, None, None]
    of_chip = jnp.arange(CHIPS, dtype=jnp.int32)[None, :, None]
    index = (of_chip * 4 * few + kinds * 2 * few + near).reshape(-1) + span_start[0]
    turn_a = tables(index + parity * few)
    turn_b = tables(index + (1 - parity) * few)
    turn_kv = tables(
        span_start[0] + chip * 4 * few + jnp.arange(4 * few, dtype=jnp.int32)
    )

    q_got = hop(lax.dynamic_slice_in_dim(q_weight, (1 - core) * width, width, 1), dc=1)
    kv_got = hop(jnp.where(core == 0, v_weight, k_weight), dc=1)
    got = (q_got, kv_got)

    mine, got, b300, b100, b010, turn_a, turn_b, turn_kv = barrier(
        (mine, got, b300, b100, b010, turn_a, turn_b, turn_kv)
    )
    far = CHIPS * few // 2
    other = [hop_y(mine[:far], 1), hop_y(mine[far:], -1)]
    mine_twin = hop(mine, dc=1)

    def sums(parts):
        return project(core, parts, q_weight, k_weight, v_weight, got).astype(jnp.float16)

    half = SPAN // 2

    def total_of(parts):
        return jnp.sum(parts.astype(jnp.float32), axis=0)

    b310 = hop(b010, dz=1)
    b200 = hop(b100, dz=-1)
    b110 = hop(b100, dx=1)
    first_own = [b000, b300, b100, b010]

    sent_a = trade(sums([mine, mine_twin]), 0)
    other, b310, b200, b110 = barrier((other, b310, b200, b110))
    other_twin = [hop(x, dc=1) for x in other]
    first_swap = [hop(b, dc=1) for b in first_own]
    q_b = sums(other + other_twin)

    cut = ROWS
    b210 = [hop(b200[:cut], dx=1), hop(b310[cut:], dz=1)]
    sum_a = total_of(sent_a)
    q_b, sum_a, first_swap, b210 = barrier((q_b, sum_a, first_swap, b210))
    sent_b = trade(q_b, 0)
    second_own = [b310, b200, b110]
    second_swap = [hop(b, dc=1) for b in second_own]

    z_me, x_me = chip // NX, chip % NX
    pieces, places, slots = [], [], []

    def add(own, swap, dz, dx, first=0, fresh=True):
        if fresh:
            place = ((z_me + dz) % NZ) * NX * NC + ((x_me + dx) % NX) * NC
            slots.extend([place + core, place + 1 - core])
        pieces.extend([own, swap])
        places.extend([(len(slots) - 2, first, dz), (len(slots) - 1, first, dz)])

    for own, swap, (dz, dx) in zip(
        first_own + second_own,
        first_swap + second_swap,
        [(0, 0), (3, 0), (1, 0), (0, 1), (3, 1), (2, 0), (1, 1)],
    ):
        add(own, swap, dz, dx)
    for i, part in enumerate(b210):
        add(part, hop(part, dc=1), 2, 1, i * cut, i == 0)
    places = tuple(places)
    meta = jnp.stack([cache_len[0], core, parity, z_me] + slots).astype(jnp.int32)

    shapes = (
        jax.ShapeDtypeStruct((HD, half), jnp.float32),
        jax.ShapeDtypeStruct((8, half), jnp.float32),
        jax.ShapeDtypeStruct((half, HD), jnp.bfloat16),
    )
    def attend(sums, turn):
        return attention_call(cache_kernel, meta, [sums, *turn], pieces, places, shapes)

    state_a = attend(sum_a, turn_a)
    sent_b, state_a = barrier((sent_b, state_a))
    sum_b = total_of(sent_b)
    state_b = attend(sum_b, turn_b)

    settled = settle(core, parity, sum_a, sum_b, *turn_kv)
    new = trade(settled, 0)
    new, state_b = barrier((new, state_b))
    mixed = attention_call(
        last_kernel,
        meta,
        [*state_a, *state_b, new, hop(new, dc=1)],
        pieces,
        places,
        jax.ShapeDtypeStruct((CHIPS, NC, 2, few, HD), jnp.bfloat16),
    )
    n_all = n_tensor * NC * CHIPS
    out_rows = SPAN // n_all
    moved = lax.all_to_all(
        mixed.reshape(n_all, out_rows, HD),
        ("tensor", "ulysses"),
        split_axis=0,
        concat_axis=0,
        tiled=True,
    )
    moved = moved.reshape(n_tensor, CHIPS, NC, out_rows, HD)
    return jnp.transpose(moved, (3, 0, 2, 1, 4)).reshape(out_rows, n_all * HD)


def solution(mesh):
    placed = (
        P("ulysses", None),
        P("ulysses", "tensor"),
        P("ulysses", "tensor"),
        P("ulysses", "tensor"),
        P("ulysses", "tensor"),
        P("ulysses", "tensor"),
        P(),
        P(),
    )
    return jax.shard_map(
        on_device,
        mesh=mesh,
        in_specs=placed,
        out_specs=P(("tensor", "ulysses"), None),
        check_vma=False,
    )
```
